256 devices in a mesh: pair: 32 (over z, y), occ: 8 (over x, core).
Axes of the slice: x: 4, y: 4, z: 8, core: 2. Of those that a mesh axis runs over, the one named last changes fastest.
Arguments:
- amplitudes: float32 [256, 128, 128], P('pair'), may hold values from -4 to 4
- exchange_ints: float32 [256, 128, 128], P('pair'), may hold values from -6 to 6
- pno_energy: float32 [256, 128], P('pair'), may hold values from 0.3 to 3
- pair_shift: float32 [256], P('pair'), may hold values from 0.5 to 2
- coefficients: bfloat16 [256, 512, 128], P('pair'), may hold values from -0.5 to 0.5
- domain_tiles: int32 [256, 4], P('pair'), may hold values from 0 to 3, each once within a row
- couple_owner: int32 [8, 256, 8, 1], P('occ', 'pair'), may hold values from 0 to 31; in each aligned block of 64 rows (0 to 63, 64 to 127, ..., all dimensions but the last counted through in order) at most 3 rows name the same one
- couple_index: int32 [8, 256, 8], P('occ', 'pair'), may hold values from 0 to 7
- couple_weight: float32 [8, 256, 8], P('occ', 'pair'), may hold values from -0.5 to 0.5
Outputs:
- final_amplitudes: float32 [256, 128, 128], P('pair')
- final_residual: float32 [256, 128, 128], P('pair')
The draws below stay inside these ranges and needn't reach their ends.
Inputs may be any that keep to these rules, and one draw needn't show every extreme that they name: `couple_owner`: among the couplings held by one device (one block of 64 entries), no owner is named more than 3 times. `domain_tiles`: the tiles of one pair's domain are distinct.
All inputs are finite; a program needn't handle non-finite values.
Results may differ from the reference program's by a relative error of at most 0.0003.
Values may be sent and summed in bfloat16 or wider, within the bound.
A program may use at most 128 MiB of HBM per device.

```python
import math
import jax
import jax.numpy as jnp
import numpy as np
from jax import lax

NPNO = 128
TILE = 128
DOM_TILES = 4
PAIR_DEV = 8
ITERS = 2
DOMAIN = 512
PAIRS = 256
NCOUP_DEV = 8
CAP = 3
N_PAIR = 32
N_OCC = 8


def place_ends(values, own_key, smallest, largest):
    shape = values.shape
    spot = [jax.random.randint(jax.random.fold_in(own_key, axis), (), 0, shape[axis]) for axis in range(len(shape))]
    values = values.at[tuple(spot)].set(smallest)
    longest = shape.index(max(shape))
    spot[longest] = (spot[longest] + 1) % shape[longest]
    return values.at[tuple(spot)].set(largest)


def steps_of(rng, extent, cuts, smallest, high):
    def one(position, shards_of):
        draws = jax.random.uniform(jax.random.fold_in(jax.random.fold_in(rng, 6), position), (shards_of,), jnp.float32, smallest / len(cuts), high / len(cuts))
        return jnp.repeat(jnp.exp(draws), extent[position] // shards_of).reshape((-1,) + (1,) * (len(extent) - position - 1))

    loudness = one(*cuts[0])
    for cut in cuts[1:]:
        loudness = loudness * one(*cut)
    return loudness


def assign_block(stream_key, own, number, rows, number_of, top, limit, lean):
    sequence = jax.random.permutation(stream_key, number_of)
    crowded, ordinary = load_shares(number_of, rows * top, limit, lean, True), load_shares(number_of, rows * top, limit, lean, False)
    places = jnp.arange(number_of)

    def named(lengths, turn):
        used = int((lengths > 0).sum())
        fixed = max(1, used // 4)
        shifted = fixed + (places - fixed + turn * (used - fixed)) % max(1, number_of - fixed)
        return jnp.zeros((number_of,), jnp.int32).at[sequence[jnp.where(places < fixed, places, shifted)]].set(jnp.asarray(lengths, jnp.int32))

    lengths = jnp.where(number % 4 == 0, named(crowded, number // 4), named(ordinary, number - number // 4 - 1))
    mixed = jax.random.permutation(jax.random.fold_in(own, 3), number_of)
    giver, taker = mixed[0:number_of // 2 * 2:2], mixed[1:number_of // 2 * 2:2]
    margin = jnp.minimum(lengths[giver] - 1, limit - lengths[taker]) // 2
    margin = jnp.where((giver == sequence[0]) | (taker == sequence[0]) | (lengths[taker] == 0), 0, jnp.maximum(margin, 0))
    shifted = jax.random.randint(jax.random.fold_in(own, 4), (number_of // 2,), 0, 1 << 20) % (margin + 1)
    lengths = lengths.at[giver].add(-shifted).at[taker].add(shifted)
    labels = jnp.searchsorted(jnp.cumsum(lengths), jnp.arange(rows * top), side="right").astype(jnp.int32)
    listing = labels.reshape(top, rows).T
    listing = listing[jax.random.permutation(jax.random.fold_in(own, 1), rows)]
    turn = jax.random.randint(jax.random.fold_in(own, 2), (rows, 1), 0, top)
    return jnp.take_along_axis(listing, (jnp.arange(top)[None, :] + turn) % top, axis=1)


def load_shares(count, total, most, slope, full):
    loads = [(1 << 20) // math.isqrt(rank ** slope) + 1 for rank in range(1, count + 1)]
    largest = most if full else min(most, max(-(-total // count), total * loads[0] // sum(loads)))
    least = 1 if total - largest >= count - 1 else 0
    holding, spare = [largest] + [least] * (count - 1), total - largest - least * (count - 1)
    while spare > 0:
        free = [i for i in range(1, count) if holding[i] < largest] or [i for i in range(1, count) if holding[i] < most]
        whole, left = sum([loads[i] for i in free]), spare
        for i in free:
            extra = min(most - holding[i], max(1, left * loads[i] // whole), spare)
            holding[i] = holding[i] + extra
            spare = spare - extra
    return np.array(holding)


def bell_draw(key, dims, width, reach, cuts=(), kind=jnp.bfloat16):
    gain = steps_of(key, dims, cuts, -0.22, 0.18) if cuts else 1.0
    values = jax.random.normal(key, dims, jnp.float32) * width * gain
    return jnp.minimum(jnp.maximum(values, -reach), reach).astype(kind)


def setup_inputs(seed: int = 0) -> dict:
    arg_keys = jax.random.split(jax.random.key(seed), 10)
    amplitudes = bell_draw(arg_keys[0], (PAIRS, NPNO, NPNO), 0.3, 4.0, ((0, 32),), jnp.float32)
    exchange_ints = bell_draw(arg_keys[1], (PAIRS, NPNO, NPNO), 1.0, 6.0, ((0, 32),), jnp.float32)
    pno_energy = jnp.clip(jnp.exp(math.log(3.0) - 2.3025851 * jax.random.uniform(arg_keys[2], (PAIRS, NPNO), jnp.float32) ** steps_of(arg_keys[2], (PAIRS, NPNO), ((0, 32),), -0.2, 0.2)), 0.3, 3.0)
    pair_shift = jnp.clip(0.5 + 1.5 * jax.random.uniform(arg_keys[3], (PAIRS,), jnp.float32) ** steps_of(arg_keys[3], (PAIRS,), ((0, 32),), -0.2, 0.2), 0.5, 2.0)
    coefficients = bell_draw(arg_keys[4], (PAIRS, DOMAIN, NPNO), TILE ** -0.5, 0.5, ((0, 32),))
    domain_tiles = jax.vmap(lambda own: jax.random.permutation(own, DOM_TILES))(jax.random.split(arg_keys[5], PAIRS)).reshape((PAIRS, DOM_TILES)).astype(jnp.int32)
    couple_owner_keys = jax.random.split(jax.random.fold_in(arg_keys[6], 1), N_OCC * PAIRS * NCOUP_DEV // (PAIR_DEV * NCOUP_DEV))
    couple_owner_turns = jax.random.permutation(jax.random.fold_in(arg_keys[6], 3), N_OCC * PAIRS * NCOUP_DEV // (PAIR_DEV * NCOUP_DEV))
    couple_owner = jax.vmap(lambda own, number: assign_block(jax.random.fold_in(arg_keys[6], 2), own, number, PAIR_DEV * NCOUP_DEV, N_PAIR, 1, CAP, 2))(couple_owner_keys, couple_owner_turns).reshape((N_OCC, PAIRS, NCOUP_DEV, 1))
    couple_index = place_ends(jax.random.randint(arg_keys[7], (N_OCC, PAIRS, NCOUP_DEV), 0, PAIR_DEV), jax.random.fold_in(arg_keys[7], 1), 0, PAIR_DEV - 1).astype(jnp.int32)
    couple_weight = bell_draw(arg_keys[8], (N_OCC, PAIRS, NCOUP_DEV), 0.08, 0.5, ((0, 8), (1, 32)), jnp.float32)
    return dict(amplitudes=amplitudes, exchange_ints=exchange_ints, pno_energy=pno_energy, pair_shift=pair_shift, coefficients=coefficients, domain_tiles=domain_tiles, couple_owner=couple_owner, couple_index=couple_index, couple_weight=couple_weight)


HIGHEST = lax.Precision.HIGHEST


def moved_onto(own_tiles, partner_tiles, partner_coef):
    total_count = partner_coef.shape[0]
    tile_match = (own_tiles[None, :, None] == partner_tiles[:, None, :]).astype(jnp.float32)
    tile_blocks = partner_coef.astype(jnp.float32).reshape(total_count, DOM_TILES, TILE * NPNO)
    moved_tiles = jnp.einsum('cab,cbx->cax', tile_match, tile_blocks, precision=HIGHEST)
    return moved_tiles.reshape(total_count, DOM_TILES * TILE, NPNO)


def reference(amplitudes, exchange_ints, pno_energy, pair_shift, coefficients, domain_tiles, couple_owner, couple_index, couple_weight):
    partner = (couple_owner[..., 0] * PAIR_DEV + couple_index).astype(jnp.int32)
    partner = jnp.transpose(partner, (1, 0, 2)).reshape(PAIRS, N_OCC * NCOUP_DEV)
    weights = jnp.transpose(couple_weight, (1, 0, 2)).reshape(PAIRS, N_OCC * NCOUP_DEV)
    denominator = pno_energy[:, :, None] + pno_energy[:, None, :] + pair_shift[:, None, None]

    def coupled(current):
        def one_pair(pair_index):
            partner_rows = partner[pair_index]
            own_coef = coefficients[pair_index].astype(jnp.float32)
            moved_tiles = moved_onto(domain_tiles[pair_index], domain_tiles[partner_rows], coefficients[partner_rows])
            intersection = jnp.einsum('fa,cfb->cab', own_coef, moved_tiles, precision=HIGHEST)
            inner_prod = jnp.einsum('cab,cbd->cad', intersection, current[partner_rows], precision=HIGHEST)
            outer_prod = jnp.einsum('cad,ced->cae', inner_prod, intersection, precision=HIGHEST)
            return jnp.einsum('c,cae->ae', weights[pair_index], outer_prod, precision=HIGHEST)
        return lax.map(one_pair, jnp.arange(PAIRS, dtype=jnp.int32))

    current = amplitudes
    residual = amplitudes
    for iteration in range(ITERS):
        residual = exchange_ints + denominator * current - coupled(current)
        current = current - residual / denominator
    return current, residual
```

```python
import jax
import jax.numpy as jnp
from jax import lax
from jax.sharding import Mesh
from jax.sharding import PartitionSpec as P

ITERS = 2
PAIR = ("pair_0", "pair_1")


def local(
    amplitudes,
    exchange_ints,
    pno_energy,
    pair_shift,
    coefficients,
    domain_tiles,
    couple_owner,
    couple_index,
    couple_weight,
):
    pairs, tiles = domain_tiles.shape
    width = amplitudes.shape[1]
    owners = couple_owner[0, :, :, 0]
    places = couple_index[0]
    weights = couple_weight[0]
    me = lax.axis_index("occ")
    peers = lax.axis_size(PAIR)
    blocks = coefficients.reshape(pairs, tiles, -1, width)
    match = domain_tiles[:, None, :] == jnp.arange(tiles, dtype=jnp.int32)[None, :, None]
    ordered = jnp.sum(
        jnp.where(match[..., None, None], blocks[:, None], jnp.zeros((), blocks.dtype)),
        axis=2,
        dtype=blocks.dtype,
    ).reshape(coefficients.shape)
    own = lax.dynamic_index_in_dim(ordered, me, 0, keepdims=False)
    theirs = lax.all_gather(own, PAIR)
    named = (owners[:, :, None] == jnp.arange(peers, dtype=jnp.int32)) * weights[:, :, None]
    place = places[:, :, None] == jnp.arange(pairs, dtype=jnp.int32)
    table = jnp.sum(named[:, :, None, :] * place[:, :, :, None], axis=1)
    table = lax.psum_scatter(table, "occ", scatter_dimension=1, tiled=True)[:, 0]
    overlap = jnp.einsum("pfa,qfb->pqab", ordered, theirs, preferred_element_type=jnp.float32)
    pick = lambda x: lax.dynamic_index_in_dim(x, me, 0, keepdims=False)
    energy, shift = pick(pno_energy), pick(pair_shift)
    denominator = energy[:, None] + energy[None, :] + shift
    current, exchange = pick(amplitudes), pick(exchange_ints)
    residual = current
    for _ in range(ITERS):
        amps = lax.all_gather(current, PAIR)
        inner = jnp.einsum("pqab,qbd->pqad", overlap, amps, precision=lax.Precision.HIGH)
        inner = inner * table[:, :, None, None]
        part = jnp.einsum("pqad,pqed->pae", inner, overlap, precision=lax.Precision.HIGH)
        coupled = lax.psum_scatter(part, "occ", scatter_dimension=0, tiled=True)[0]
        residual = exchange + denominator * current - coupled
        current = current - residual / denominator
    return lax.all_gather(current, "occ"), lax.all_gather(residual, "occ")


def solution(mesh):
    split = Mesh(mesh.devices.reshape(8, 4, mesh.shape["occ"]), ("pair_0", "pair_1", "occ"))
    in_specs = (
        P(PAIR, None, None),
        P(PAIR, None, None),
        P(PAIR, None),
        P(PAIR),
        P(PAIR, None, None),
        P(PAIR, None),
        P("occ", PAIR, None, None),
        P("occ", PAIR, None),
        P("occ", PAIR, None),
    )
    out_specs = (P(PAIR, None, None), P(PAIR, None, None))
    return jax.shard_map(local, mesh=split, in_specs=in_specs, out_specs=out_specs, check_vma=False)
```

```python
import jax
import jax.numpy as jnp
from jax import lax
from jax.experimental import pallas as pl
from jax.experimental.pallas import tpu as pltpu
from jax.sharding import Mesh
from jax.sharding import PartitionSpec as P

F32, BF16 = jnp.float32, jnp.bfloat16
NZ, NY, NX, NC = 8, 4, 4, 2
OWNERS, PEERS = NZ * NY, NX * NC
N = 128
TILES = 4
DOMAIN = TILES * N
PAIRS = 8
ROWS = PAIRS * N
CHUNK = 512
AXES = ("z", "y", "x", "core")
PAIR, OCC = ("z", "y"), ("x", "core")


def split(x):
    high = x.astype(BF16)
    return high, (x - high.astype(F32)).astype(BF16)


def push(src, dst, send, recv, device):
    return pltpu.make_async_remote_copy(
        src_ref=src, dst_ref=dst, send_sem=send, recv_sem=recv,
        device_id=device, device_id_type=pl.DeviceIdType.MESH,
    )


class Place:
    def __init__(self):
        self.z, self.y = lax.axis_index("z"), lax.axis_index("y")
        self.occ = lax.axis_index("x") * NC + lax.axis_index("core")
        self.me = self.z * NY + self.y

    def z_to(self, d):
        return {"z": lax.rem(self.z + d + NZ, NZ)}

    def y_to(self, d):
        return {"y": lax.rem(self.y + d + NY, NY)}

    def peer(self, j):
        other = lax.rem(self.occ + j + PEERS, PEERS)
        return other, {"x": other // NC, "core": lax.rem(other, NC)}

    def sign(self, k):
        return 2 * lax.rem(k, 2) - 1

    def row(self, k):
        return lax.rem(self.z + self.sign(k) * ((k + 1) // 2) + NZ, NZ)

    def slot(self, k, dy):
        return self.row(k) * NY + lax.rem(self.y + dy + NY, NY)


class Gather:
    def __init__(self, at, buf, base, rows, zs, zr, ys, yr):
        self.at, self.buf, self.base, self.rows = at, buf, base, rows
        self.zs, self.zr, self.ys, self.yr = zs, zr, ys, yr

    def piece(self, slot, half):
        n = self.rows if half is None else self.rows // 2
        return self.buf.at[slot, pl.ds(self.base + (n if half == 1 else 0), n)]

    def copy(self, axis, slot, half, index, d):
        part = self.piece(slot, half)
        if axis == "z":
            return push(part, part, self.zs.at[index], self.zr.at[index], self.at.z_to(d))
        return push(part, part, self.ys.at[index], self.yr.at[index], self.at.y_to(d))

    def along_z(self, k, slot, tail):
        at, d = self.at, -self.at.sign(k)

        @pl.when(k < 7)
        def _():
            self.copy("z", slot, None, (k,) + tail, d).wait_recv()

        @pl.when(k < 5)
        def _():
            self.copy("z", slot, None, (k + 2,) + tail, d).start()

        @pl.when(k == 5)
        def _():
            self.copy("z", slot, 0, (7,) + tail, -1).start()

        @pl.when(k == 6)
        def _():
            self.copy("z", slot, 1, (8,) + tail, 1).start()

        @pl.when(k == 7)
        def _():
            self.copy("z", slot, 0, (7,) + tail, -1).wait_recv()
            self.copy("z", slot, 1, (8,) + tail, 1).wait_recv()

    def both_z(self, slot, tail):
        self.copy("z", slot, None, (1,) + tail, -1).start()
        self.copy("z", slot, None, (2,) + tail, 1).start()

    def sent_z(self, tail):
        for k in range(1, 7):
            self.copy("z", 0, None, (k,) + tail, 1).wait_send()
        self.copy("z", 0, 0, (7,) + tail, 1).wait_send()
        self.copy("z", 0, 1, (8,) + tail, 1).wait_send()


class ZFirst(Gather):
    def start(self):
        self.both_z(self.at.me, ())
        self.both_y(0)

    def both_y(self, k):
        slot = self.at.slot(k, 0)
        self.copy("y", slot, None, (k, 0), -1).start()
        self.copy("y", slot, None, (k, 1), 1).start()

    def take_z(self, k):
        self.along_z(k, self.at.slot(k, 0), ())
        self.both_y(k)

    def take_y(self, k):
        slot = self.at.slot(k, 1)
        self.copy("y", slot, None, (k, 0), -1).wait_recv()
        self.copy("y", slot, 0, (k, 2), -1).start()
        slot = self.at.slot(k, -1)
        self.copy("y", slot, None, (k, 1), 1).wait_recv()
        self.copy("y", slot, 1, (k, 3), 1).start()

    def last_y(self, k):
        slot = self.at.slot(k, 2)
        self.copy("y", slot, 0, (k, 2), -1).wait_recv()
        self.copy("y", slot, 1, (k, 3), 1).wait_recv()

    def sent(self):
        self.sent_z(())

        @pl.loop(0, NZ)
        def _(k):
            for index, half in enumerate((None, None, 0, 1)):
                self.copy("y", 0, half, (k, index), 1).wait_send()


class YFirst(Gather):
    def start(self):
        me = self.at.me
        self.copy("y", me, None, (0,), -1).start()
        self.copy("y", me, None, (1,), 1).start()
        self.both_z(me, (0,))

    def take_y(self):
        slot = self.at.slot(0, 1)
        self.copy("y", slot, None, (0,), -1).wait_recv()
        self.copy("y", slot, 0, (2,), -1).start()
        self.both_z(slot, (1,))
        slot = self.at.slot(0, -1)
        self.copy("y", slot, None, (1,), 1).wait_recv()
        self.copy("y", slot, 1, (3,), 1).start()
        self.both_z(slot, (2,))
        slot = self.at.slot(0, 2)
        self.copy("y", slot, 0, (2,), -1).wait_recv()
        self.copy("y", slot, 1, (3,), 1).wait_recv()
        self.both_z(slot, (3,))

    def take_z(self, k):
        for j, dy in enumerate((0, 1, -1, 2)):
            self.along_z(k, self.at.slot(k, dy), (j,))

    def sent(self):
        for index, half in enumerate((None, None, 0, 1)):
            self.copy("y", 0, half, (index,), 1).wait_send()
        for j in range(NY):
            self.sent_z((j,))


class Spread:
    def __init__(self, at, out, into, send, recv):
        self.at, self.out, self.into, self.send, self.recv = at, out, into, send, recv

    def copy(self, j):
        other, device = self.at.peer(j)
        return push(self.out(other), self.into.at[self.at.occ], self.send.at[j], self.recv.at[j], device)

    def start(self):
        for j in range(1, PEERS):
            self.copy(j).start()

    def arrived(self):
        for j in range(1, PEERS):
            self.copy(j).wait_recv()

    def sent(self):
        for j in range(1, PEERS):
            self.copy(j).wait_send()


def kernel(
    amp_hbm, exch_hbm, energy_ref, shift_ref, coef_ref, tiles_ref, pair_ref, weight_ref,
    final_ref, residual_ref,
    flipped, coef_all, amp_all, amp_next, high, low, inner, total,
    sums, sums_next, current_all, residual_all, table_out, table_in, table,
    amp_own, exch_own,
    own_sem, c_zs, c_zr, c_ys, c_yr, t_zs, t_zr, t_ys, t_yr,
    n_zs, n_zr, n_ys, n_yr, m_zs, m_zr, m_ys, m_yr, peer_send, peer_recv,
):
    at = Place()
    fetch = [
        pltpu.make_async_copy(amp_hbm.at[at.occ], amp_own, own_sem.at[0]),
        pltpu.make_async_copy(exch_hbm.at[at.occ], exch_own, own_sem.at[1]),
    ]
    for copy in fetch:
        copy.start()

    barrier = pltpu.get_barrier_semaphore()
    for device in (at.z_to(-1), at.z_to(1), at.y_to(-1), at.y_to(1)):
        pl.semaphore_signal(barrier, inc=1, device_id=device, device_id_type=pl.DeviceIdType.MESH)
    for j in range(1, PEERS):
        pl.semaphore_signal(barrier, inc=1, device_id=at.peer(j)[1], device_id_type=pl.DeviceIdType.MESH)

    def ordered(p, t):
        tile = jnp.zeros((N, N), F32)
        for b in range(TILES):
            same = jnp.where(tiles_ref[p, b] == t, 1.0, 0.0)
            tile += coef_ref[p, b * N : (b + 1) * N, :].astype(F32) * same
        return tile.astype(BF16)

    for t in range(TILES):
        coef_all[at.me, t * N : (t + 1) * N, :] = ordered(at.occ, t)
    lane = lax.broadcasted_iota(jnp.int32, (PAIRS, N), 1) * PAIRS
    for place in range(PAIRS):
        piece = jnp.zeros((PAIRS, N), F32)
        for c in range(pair_ref.shape[1]):
            named = jnp.broadcast_to(pair_ref[:, c : c + 1], (PAIRS, N)) == lane + place
            piece += jnp.where(named, jnp.broadcast_to(weight_ref[:, c : c + 1], (PAIRS, N)), 0.0)
        table_out[place] = piece
    table_in[at.occ] = table_out[at.occ]
    for copy in fetch:
        copy.wait()
    amp_all[at.me] = amp_own[...]
    pl.semaphore_wait(barrier, 4 + PEERS - 1)

    coefs = ZFirst(at, coef_all, 0, DOMAIN, c_zs, c_zr, c_ys, c_yr)
    amps = YFirst(at, amp_all, 0, N, t_zs, t_zr, t_ys, t_yr)
    tables = Spread(at, lambda other: table_out.at[other], table_in, peer_send.at[0], peer_recv.at[0])
    coefs.start()
    amps.start()
    tables.start()

    @pl.loop(0, PAIRS)
    def _(p):
        for t in range(TILES):
            flipped[pl.ds(p * N, N), t * N : (t + 1) * N] = ordered(p, t).T

    tables.arrived()
    weights = table_in[0]
    for other in range(1, PEERS):
        weights += table_in[other]
    for owner in range(OWNERS):
        table[owner] = jnp.broadcast_to(weights[:, owner : owner + 1], (PAIRS, N))
    amps.take_y()

    def overlaps(base):
        for pair in range(0, NY, 2):
            theirs = jnp.concatenate([coef_all[base + pair], coef_all[base + pair + 1]], axis=1)
            for first in range(0, ROWS, CHUNK):
                rows = slice(first, first + CHUNK)
                s = jnp.dot(flipped[rows, :], theirs, preferred_element_type=F32)
                up, down = split(s)
                for i in range(2):
                    high[base + pair + i, rows, :] = up[:, i * N : (i + 1) * N]
                    low[base + pair + i, rows, :] = down[:, i * N : (i + 1) * N]

    def couple(base, amplitudes):
        for y in range(NY):
            slot = base + y
            both = jnp.concatenate(split(amplitudes[slot]), axis=1)
            both = jnp.concatenate([both, both], axis=0)
            for first in range(0, ROWS, CHUNK):
                rows = slice(first, first + CHUNK)
                s = jnp.concatenate([high[slot, rows, :], low[slot, rows, :]], axis=1)
                u = jnp.dot(s, both, preferred_element_type=F32)
                u = (u[:, :N] + u[:, N:]).reshape(CHUNK // N, N, N)
                u = u * table[slot, first // N : (first + CHUNK) // N, :][:, None, :]
                up, down = split(u.reshape(CHUNK, N))
                inner[y, rows, :N] = up
                inner[y, rows, N:] = down

        @pl.loop(0, PAIRS)
        def _(p):
            rows = pl.ds(pl.multiple_of(p * N, N), N)
            left = jnp.concatenate([inner[y, rows, :] for y in range(NY)], axis=1)
            right = []
            for y in range(NY):
                up, down = high[base + y, rows, :], low[base + y, rows, :]
                right.append(jnp.concatenate([up, down], axis=0))
                right.append(right[-1])
            out = lax.dot_general(
                left, jnp.concatenate(right, axis=1), (((1,), (1,)), ((), ())),
                preferred_element_type=F32,
            )
            total[p] += out[:, :N] + out[:, N:]

    def denominator(p):
        line = jnp.broadcast_to(energy_ref[pl.ds(p, 1), :], (N, N))
        return line.T + line + shift_ref[p]

    def gathered(into, index):
        spread = Spread(at, lambda other: total.at[other], into, peer_send.at[index], peer_recv.at[index])
        spread.start()
        spread.arrived()
        coupled = total[at.occ]
        for j in range(1, PEERS):
            coupled += into[at.peer(-j)[0]]
        spread.sent()
        return coupled

    total[...] = jnp.zeros_like(total)

    @pl.loop(0, NZ)
    def _(k):
        @pl.when(k < NZ - 1)
        def _():
            coefs.take_z(k + 1)

        coefs.take_y(k)

        @pl.when(k < NZ - 1)
        def _():
            amps.take_z(k + 1)

        coefs.last_y(k)
        base = at.row(k) * NY
        overlaps(base)
        couple(base, amp_all)

    coupled = gathered(sums, 1)
    below = denominator(at.occ)
    current = amp_own[...]
    current = current - (exch_own[...] + below * current - coupled) / below
    amp_next[at.me] = current
    current_all[at.occ] = current
    total[...] = jnp.zeros_like(total)

    late = ZFirst(at, amp_next, N // 2, N // 2, m_zs, m_zr, m_ys, m_yr)
    early = YFirst(at, amp_next, 0, N // 2, n_zs, n_zr, n_ys, n_yr)
    currents = Spread(at, lambda other: current_all.at[at.occ], current_all, peer_send.at[2], peer_recv.at[2])
    late.start()
    early.start()
    early.take_y()
    currents.start()

    @pl.loop(0, NZ)
    def _(k):
        @pl.when(k < NZ - 1)
        def _():
            late.take_z(k + 1)

        late.take_y(k)

        @pl.when(k < NZ - 1)
        def _():
            early.take_z(k + 1)

        late.last_y(k)
        couple(at.row(k) * NY, amp_next)

    coupled = gathered(sums_next, 3)
    current = current_all[at.occ]
    residual_all[at.occ] = exch_own[...] + below * current - coupled
    residuals = Spread(at, lambda other: residual_all.at[at.occ], residual_all, peer_send.at[4], peer_recv.at[4])
    residuals.start()
    currents.arrived()
    residuals.arrived()

    @pl.loop(0, PAIRS)
    def _(p):
        residual = residual_all[p]
        residual_ref[p] = residual
        final_ref[p] = current_all[p] - residual / denominator(p)

    for copies in (coefs, amps, tables, late, early, currents, residuals):
        copies.sent()


def gather_sems():
    dma = pltpu.SemaphoreType.DMA
    z_first = [dma((9,)), dma((9,)), dma((NZ, 4)), dma((NZ, 4))]
    y_first = [dma((9, NY)), dma((9, NY)), dma((4,)), dma((4,))]
    return z_first + y_first + y_first + z_first


def local(
    amplitudes,
    exchange_ints,
    pno_energy,
    pair_shift,
    coefficients,
    domain_tiles,
    couple_owner,
    couple_index,
    couple_weight,
):
    coupled_pair = couple_owner[0, :, :, 0] * PAIRS + couple_index[0]
    vmem, smem, hbm = (
        pl.BlockSpec(memory_space=s) for s in (pltpu.VMEM, pltpu.SMEM, pl.ANY)
    )
    block = (N, N)
    out = jax.ShapeDtypeStruct((PAIRS, N, N), F32)
    return pl.pallas_call(
        kernel,
        out_shape=(out, out),
        in_specs=[hbm, hbm, vmem, smem, vmem, smem, vmem, vmem],
        out_specs=(vmem, vmem),
        scratch_shapes=[
            pltpu.VMEM((ROWS, DOMAIN), BF16),
            pltpu.VMEM((OWNERS, DOMAIN, N), BF16),
            pltpu.VMEM((OWNERS,) + block, F32),
            pltpu.VMEM((OWNERS,) + block, F32),
            pltpu.VMEM((OWNERS, ROWS, N), BF16),
            pltpu.VMEM((OWNERS, ROWS, N), BF16),
            pltpu.VMEM((NY, ROWS, 2 * N), BF16),
            pltpu.VMEM((PAIRS,) + block, F32),
            pltpu.VMEM((PEERS,) + block, F32),
            pltpu.VMEM((PEERS,) + block, F32),
            pltpu.VMEM((PAIRS,) + block, F32),
            pltpu.VMEM((PAIRS,) + block, F32),
            pltpu.VMEM((PEERS, PAIRS, N), F32),
            pltpu.VMEM((PEERS, PAIRS, N), F32),
            pltpu.VMEM((OWNERS, PAIRS, N), F32),
            pltpu.VMEM(block, F32),
            pltpu.VMEM(block, F32),
            pltpu.SemaphoreType.DMA((2,)),
            *gather_sems(),
            pltpu.SemaphoreType.DMA((5, PEERS)),
            pltpu.SemaphoreType.DMA((5, PEERS)),
        ],
        compiler_params=pltpu.CompilerParams(
            collective_id=0, has_side_effects=True, vmem_limit_bytes=52 << 20
        ),
    )(
        amplitudes, exchange_ints, pno_energy, pair_shift, coefficients, domain_tiles,
        coupled_pair, couple_weight[0],
    )


def solution(mesh):
    grid = Mesh(mesh.devices.reshape(NZ, NY, NX, NC), AXES)
    in_specs = (
        P(PAIR, None, None),
        P(PAIR, None, None),
        P(PAIR, None),
        P(PAIR),
        P(PAIR, None, None),
        P(PAIR, None),
        P(OCC, PAIR, None, None),
        P(OCC, PAIR, None),
        P(OCC, PAIR, None),
    )
    out_specs = (P(PAIR, None, None), P(PAIR, None, None))
    return jax.shard_map(local, mesh=grid, in_specs=in_specs, out_specs=out_specs, check_vma=False)
```

```python
import jax
import jax.numpy as jnp
from jax import lax
from jax.experimental import pallas as pl
from jax.experimental.pallas import tpu as pltpu
from jax.sharding import Mesh
from jax.sharding import PartitionSpec as P

F32, BF16 = jnp.float32, jnp.bfloat16
NZ, NY, NX, NC = 8, 4, 4, 2
OWNERS, PEERS = NZ * NY, NX * NC
N = 128
TILES = 4
DOMAIN = TILES * N
PAIRS = 8
ROWS = PAIRS * N
CHUNK = 512
AXES = ("z", "y", "x", "core")
PAIR, OCC = ("z", "y"), ("x", "core")


def split(x):
    high = x.astype(BF16)
    return high, (x - high.astype(F32)).astype(BF16)


def push(src, dst, send, recv, device):
    return pltpu.make_async_remote_copy(
        src_ref=src, dst_ref=dst, send_sem=send, recv_sem=recv,
        device_id=device, device_id_type=pl.DeviceIdType.MESH,
    )


class Place:
    def __init__(self):
        self.z, self.y = lax.axis_index("z"), lax.axis_index("y")
        self.occ = lax.axis_index("x") * NC + lax.axis_index("core")
        self.me = self.z * NY + self.y

    def z_to(self, d):
        return {"z": lax.rem(self.z + d + NZ, NZ)}

    def y_to(self, d):
        return {"y": lax.rem(self.y + d + NY, NY)}

    def peer(self, j):
        other = lax.rem(self.occ + j + PEERS, PEERS)
        return other, {"x": other // NC, "core": lax.rem(other, NC)}

    def sign(self, k):
        return 2 * lax.rem(k, 2) - 1

    def row(self, k):
        return lax.rem(self.z + self.sign(k) * ((k + 1) // 2) + NZ, NZ)

    def slot(self, k, dy):
        return self.row(k) * NY + lax.rem(self.y + dy + NY, NY)


class Gather:
    def __init__(self, at, buf, base, rows, zs, zr, ys, yr):
        self.at, self.buf, self.base, self.rows = at, buf, base, rows
        self.zs, self.zr, self.ys, self.yr = zs, zr, ys, yr

    def piece(self, slot, half):
        n = self.rows if half is None else self.rows // 2
        return self.buf.at[slot, pl.ds(self.base + (n if half == 1 else 0), n)]

    def copy(self, axis, slot, half, index, d):
        part = self.piece(slot, half)
        if axis == "z":
            return push(part, part, self.zs.at[index], self.zr.at[index], self.at.z_to(d))
        return push(part, part, self.ys.at[index], self.yr.at[index], self.at.y_to(d))

    def along_z(self, k, slot, tail):
        at, d = self.at, -self.at.sign(k)

        @pl.when(k < 7)
        def _():
            self.copy("z", slot, None, (k,) + tail, d).wait_recv()

        @pl.when(k < 5)
        def _():
            self.copy("z", slot, None, (k + 2,) + tail, d).start()

        @pl.when(k == 5)
        def _():
            self.copy("z", slot, 0, (7,) + tail, -1).start()

        @pl.when(k == 6)
        def _():
            self.copy("z", slot, 1, (8,) + tail, 1).start()

        @pl.when(k == 7)
        def _():
            self.copy("z", slot, 0, (7,) + tail, -1).wait_recv()
            self.copy("z", slot, 1, (8,) + tail, 1).wait_recv()

    def both_z(self, slot, tail):
        self.copy("z", slot, None, (1,) + tail, -1).start()
        self.copy("z", slot, None, (2,) + tail, 1).start()

    def sent_z(self, tail):
        for k in range(1, 7):
            self.copy("z", 0, None, (k,) + tail, 1).wait_send()
        self.copy("z", 0, 0, (7,) + tail, 1).wait_send()
        self.copy("z", 0, 1, (8,) + tail, 1).wait_send()


class ZFirst(Gather):
    def start(self):
        self.both_z(self.at.me, ())
        self.both_y(0)

    def both_y(self, k):
        slot = self.at.slot(k, 0)
        self.copy("y", slot, None, (k, 0), -1).start()
        self.copy("y", slot, None, (k, 1), 1).start()

    def take_z(self, k):
        self.along_z(k, self.at.slot(k, 0), ())
        self.both_y(k)

    def take_y(self, k):
        slot = self.at.slot(k, 1)
        self.copy("y", slot, None, (k, 0), -1).wait_recv()
        self.copy("y", slot, 0, (k, 2), -1).start()
        slot = self.at.slot(k, -1)
        self.copy("y", slot, None, (k, 1), 1).wait_recv()
        self.copy("y", slot, 1, (k, 3), 1).start()

    def last_y(self, k):
        slot = self.at.slot(k, 2)
        self.copy("y", slot, 0, (k, 2), -1).wait_recv()
        self.copy("y", slot, 1, (k, 3), 1).wait_recv()

    def sent(self):
        self.sent_z(())

        @pl.loop(0, NZ)
        def _(k):
            for index, half in enumerate((None, None, 0, 1)):
                self.copy("y", 0, half, (k, index), 1).wait_send()


class YFirst(Gather):
    def start(self):
        me = self.at.me
        self.copy("y", me, None, (0,), -1).start()
        self.copy("y", me, None, (1,), 1).start()
        self.both_z(me, (0,))

    def take_y(self):
        slot = self.at.slot(0, 1)
        self.copy("y", slot, None, (0,), -1).wait_recv()
        self.copy("y", slot, 0, (2,), -1).start()
        self.both_z(slot, (1,))
        slot = self.at.slot(0, -1)
        self.copy("y", slot, None, (1,), 1).wait_recv()
        self.copy("y", slot, 1, (3,), 1).start()
        self.both_z(slot, (2,))
        slot = self.at.slot(0, 2)
        self.copy("y", slot, 0, (2,), -1).wait_recv()
        self.copy("y", slot, 1, (3,), 1).wait_recv()
        self.both_z(slot, (3,))

    def take_z(self, k):
        for j, dy in enumerate((0, 1, -1, 2)):
            self.along_z(k, self.at.slot(k, dy), (j,))

    def sent(self):
        for index, half in enumerate((None, None, 0, 1)):
            self.copy("y", 0, half, (index,), 1).wait_send()
        for j in range(NY):
            self.sent_z((j,))


class Spread:
    def __init__(self, at, out, into, send, recv):
        self.at, self.out, self.into, self.send, self.recv = at, out, into, send, recv

    def copy(self, j):
        other, device = self.at.peer(j)
        return push(self.out(other), self.into.at[self.at.occ], self.send.at[j], self.recv.at[j], device)

    def start(self):
        for j in range(1, PEERS):
            self.copy(j).start()

    def arrived(self):
        for j in range(1, PEERS):
            self.copy(j).wait_recv()

    def sent(self):
        for j in range(1, PEERS):
            self.copy(j).wait_send()


def kernel(
    amp_hbm, exch_hbm, energy_ref, shift_ref, coef_ref, tiles_ref, pair_ref, weight_ref,
    final_ref, residual_ref,
    flipped, straight, coef_all, turned, amp_all, amp_next, high, low, high_t, low_t, up_all, down_all, total,
    sums, sums_next, current_all, residual_all, table_out, table_in, table,
    amp_own, exch_own,
    own_sem, c_zs, c_zr, c_ys, c_yr, t_zs, t_zr, t_ys, t_yr,
    n_zs, n_zr, n_ys, n_yr, m_zs, m_zr, m_ys, m_yr, peer_send, peer_recv,
):
    at = Place()
    fetch = [
        pltpu.make_async_copy(amp_hbm.at[at.occ], amp_own, own_sem.at[0]),
        pltpu.make_async_copy(exch_hbm.at[at.occ], exch_own, own_sem.at[1]),
    ]
    for copy in fetch:
        copy.start()

    barrier = pltpu.get_barrier_semaphore()
    for device in (at.z_to(-1), at.z_to(1), at.y_to(-1), at.y_to(1)):
        pl.semaphore_signal(barrier, inc=1, device_id=device, device_id_type=pl.DeviceIdType.MESH)
    for j in range(1, PEERS):
        pl.semaphore_signal(barrier, inc=1, device_id=at.peer(j)[1], device_id_type=pl.DeviceIdType.MESH)

    def ordered(p, t):
        tile = jnp.zeros((N, N), F32)
        for b in range(TILES):
            same = jnp.where(tiles_ref[p, b] == t, 1.0, 0.0)
            tile += coef_ref[p, b * N : (b + 1) * N, :].astype(F32) * same
        return tile.astype(BF16)

    for t in range(TILES):
        coef_all[at.me, t * N : (t + 1) * N, :] = ordered(at.occ, t)
    lane = lax.broadcasted_iota(jnp.int32, (PAIRS, N), 1) * PAIRS
    for place in range(PAIRS):
        piece = jnp.zeros((PAIRS, N), F32)
        for c in range(pair_ref.shape[1]):
            named = jnp.broadcast_to(pair_ref[:, c : c + 1], (PAIRS, N)) == lane + place
            piece += jnp.where(named, jnp.broadcast_to(weight_ref[:, c : c + 1], (PAIRS, N)), 0.0)
        table_out[place] = piece
    table_in[at.occ] = table_out[at.occ]
    for copy in fetch:
        copy.wait()
    amp_all[at.me] = amp_own[...]
    pl.semaphore_wait(barrier, 4 + PEERS - 1)

    coefs = ZFirst(at, coef_all, 0, DOMAIN, c_zs, c_zr, c_ys, c_yr)
    amps = YFirst(at, amp_all, 0, N, t_zs, t_zr, t_ys, t_yr)
    tables = Spread(at, lambda other: table_out.at[other], table_in, peer_send.at[0], peer_recv.at[0])
    coefs.start()
    amps.start()
    tables.start()

    @pl.loop(0, PAIRS)
    def _(p):
        for t in range(TILES):
            tile = ordered(p, t)
            straight[t * N : (t + 1) * N, pl.ds(pl.multiple_of(p * N, N), N)] = tile
            flipped[pl.ds(pl.multiple_of(p * N, N), N), t * N : (t + 1) * N] = tile.T

    coefs.take_z(1)
    coefs.take_z(2)
    amps.take_y()
    coefs.take_y(0)
    amps.take_z(1)
    amps.take_z(2)
    tables.arrived()
    weights = table_in[0]
    for other in range(1, PEERS):
        weights += table_in[other]
    for owner in range(OWNERS):
        table[owner] = jnp.broadcast_to(weights[:, owner : owner + 1], (PAIRS, N))

    def overlaps(base):
        for pair in range(0, NY, 2):
            theirs = jnp.concatenate([coef_all[base + pair], coef_all[base + pair + 1]], axis=1)
            for first in range(0, ROWS, CHUNK):
                rows = slice(first, first + CHUNK)
                s = jnp.dot(flipped[rows, :], theirs, preferred_element_type=F32)
                up, down = split(s)
                for i in range(2):
                    high[base + pair + i, rows, :] = up[:, i * N : (i + 1) * N]
                    low[base + pair + i, rows, :] = down[:, i * N : (i + 1) * N]
        for y in range(NY):
            for t in range(TILES):
                part = slice(t * N, (t + 1) * N)
                turned[y * N : (y + 1) * N, part] = coef_all[base + y, part, :].T
        theirs = pl.ds(pl.multiple_of(base * N, NY * N), NY * N)
        for first in range(0, ROWS, 2 * N):
            cols = slice(first, first + 2 * N)
            s = jnp.dot(turned[...], straight[:, cols], preferred_element_type=F32)
            high_t[theirs, cols], low_t[theirs, cols] = split(s)

    def couple(base, amplitudes):
        for y in range(NY):
            slot = base + y
            both = jnp.concatenate(split(amplitudes[slot]), axis=1)
            both = jnp.concatenate([both, both], axis=0)
            for first in range(0, ROWS, CHUNK):
                rows = slice(first, first + CHUNK)
                s = jnp.concatenate([high[slot, rows, :], low[slot, rows, :]], axis=1)
                u = jnp.dot(s, both, preferred_element_type=F32)
                u = (u[:, :N] + u[:, N:]).reshape(CHUNK // N, N, N)
                u = u * table[slot, first // N : (first + CHUNK) // N, :][:, None, :]
                up, down = split(u.reshape(CHUNK, N))
                up_all[rows, y * N : (y + 1) * N] = up
                down_all[rows, y * N : (y + 1) * N] = down
        theirs = pl.ds(pl.multiple_of(base * N, NY * N), NY * N)

        @pl.loop(0, PAIRS)
        def _(p):
            own = pl.ds(pl.multiple_of(p * N, N), N)
            left = jnp.concatenate([up_all[own, :], down_all[own, :]], axis=0)
            right = jnp.concatenate([high_t[theirs, own], low_t[theirs, own]], axis=1)
            out = jnp.dot(left, right, preferred_element_type=F32)
            out = out[:N] + out[N:]
            total[p] += out[:, :N] + out[:, N:]

    def denominator(p):
        line = jnp.broadcast_to(energy_ref[pl.ds(p, 1), :], (N, N))
        return line.T + line + shift_ref[p]

    def gathered(into, index):
        spread = Spread(at, lambda other: total.at[other], into, peer_send.at[index], peer_recv.at[index])
        spread.start()
        spread.arrived()
        coupled = total[at.occ]
        for j in range(1, PEERS):
            coupled += into[at.peer(-j)[0]]
        spread.sent()
        return coupled

    total[...] = jnp.zeros_like(total)

    @pl.loop(0, NZ)
    def _(k):
        @pl.when(k + 3 < NZ)
        def _():
            coefs.take_z(k + 3)

        @pl.when(k + 1 < NZ)
        def _():
            coefs.take_y(k + 1)

        @pl.when(k + 3 < NZ)
        def _():
            amps.take_z(k + 3)

        coefs.last_y(k)
        base = at.row(k) * NY
        overlaps(base)
        couple(base, amp_all)

    coupled = gathered(sums, 1)
    below = denominator(at.occ)
    current = amp_own[...]
    current = current - (exch_own[...] + below * current - coupled) / below
    amp_next[at.me] = current
    current_all[at.occ] = current
    total[...] = jnp.zeros_like(total)

    late = ZFirst(at, amp_next, N // 2, N // 2, m_zs, m_zr, m_ys, m_yr)
    early = YFirst(at, amp_next, 0, N // 2, n_zs, n_zr, n_ys, n_yr)
    currents = Spread(at, lambda other: current_all.at[at.occ], current_all, peer_send.at[2], peer_recv.at[2])
    late.start()
    early.start()
    currents.start()
    late.take_z(1)
    late.take_z(2)
    early.take_y()
    late.take_y(0)
    early.take_z(1)
    early.take_z(2)

    @pl.loop(0, NZ)
    def _(k):
        @pl.when(k + 3 < NZ)
        def _():
            late.take_z(k + 3)

        @pl.when(k + 1 < NZ)
        def _():
            late.take_y(k + 1)

        @pl.when(k + 3 < NZ)
        def _():
            early.take_z(k + 3)

        late.last_y(k)
        couple(at.row(k) * NY, amp_next)

    coupled = gathered(sums_next, 3)
    current = current_all[at.occ]
    residual_all[at.occ] = exch_own[...] + below * current - coupled
    residuals = Spread(at, lambda other: residual_all.at[at.occ], residual_all, peer_send.at[4], peer_recv.at[4])
    residuals.start()

    @pl.loop(0, PAIRS)
    def _(p):
        final_ref[p] = denominator(p)

    currents.arrived()
    residuals.arrived()

    @pl.loop(0, PAIRS)
    def _(p):
        residual = residual_all[p]
        residual_ref[p] = residual
        final_ref[p] = current_all[p] - residual / final_ref[p]

    for copies in (coefs, amps, tables, late, early, currents, residuals):
        copies.sent()


def gather_sems():
    dma = pltpu.SemaphoreType.DMA
    z_first = [dma((9,)), dma((9,)), dma((NZ, 4)), dma((NZ, 4))]
    y_first = [dma((9, NY)), dma((9, NY)), dma((4,)), dma((4,))]
    return z_first + y_first + y_first + z_first


def local(
    amplitudes,
    exchange_ints,
    pno_energy,
    pair_shift,
    coefficients,
    domain_tiles,
    couple_owner,
    couple_index,
    couple_weight,
):
    coupled_pair = couple_owner[0, :, :, 0] * PAIRS + couple_index[0]
    vmem, smem, hbm = (
        pl.BlockSpec(memory_space=s) for s in (pltpu.VMEM, pltpu.SMEM, pl.ANY)
    )
    block = (N, N)
    out = jax.ShapeDtypeStruct((PAIRS, N, N), F32)
    return pl.pallas_call(
        kernel,
        out_shape=(out, out),
        in_specs=[hbm, hbm, vmem, smem, vmem, smem, vmem, vmem],
        out_specs=(vmem, vmem),
        scratch_shapes=[
            pltpu.VMEM((ROWS, DOMAIN), BF16),
            pltpu.VMEM((DOMAIN, ROWS), BF16),
            pltpu.VMEM((OWNERS, DOMAIN, N), BF16),
            pltpu.VMEM((NY * N, DOMAIN), BF16),
            pltpu.VMEM((OWNERS,) + block, F32),
            pltpu.VMEM((OWNERS,) + block, F32),
            pltpu.VMEM((OWNERS, ROWS, N), BF16),
            pltpu.VMEM((OWNERS, ROWS, N), BF16),
            pltpu.VMEM((OWNERS * N, ROWS), BF16),
            pltpu.VMEM((OWNERS * N, ROWS), BF16),
            pltpu.VMEM((ROWS, NY * N), BF16),
            pltpu.VMEM((ROWS, NY * N), BF16),
            pltpu.VMEM((PAIRS,) + block, F32),
            pltpu.VMEM((PEERS,) + block, F32),
            pltpu.VMEM((PEERS,) + block, F32),
            pltpu.VMEM((PAIRS,) + block, F32),
            pltpu.VMEM((PAIRS,) + block, F32),
            pltpu.VMEM((PEERS, PAIRS, N), F32),
            pltpu.VMEM((PEERS, PAIRS, N), F32),
            pltpu.VMEM((OWNERS, PAIRS, N), F32),
            pltpu.VMEM(block, F32),
            pltpu.VMEM(block, F32),
            pltpu.SemaphoreType.DMA((2,)),
            *gather_sems(),
            pltpu.SemaphoreType.DMA((5, PEERS)),
            pltpu.SemaphoreType.DMA((5, PEERS)),
        ],
        compiler_params=pltpu.CompilerParams(
            collective_id=0, has_side_effects=True, vmem_limit_bytes=58 << 20
        ),
    )(
        amplitudes, exchange_ints, pno_energy, pair_shift, coefficients, domain_tiles,
        coupled_pair, couple_weight[0],
    )


def solution(mesh):
    grid = Mesh(mesh.devices.reshape(NZ, NY, NX, NC), AXES)
    in_specs = (
        P(PAIR, None, None),
        P(PAIR, None, None),
        P(PAIR, None),
        P(PAIR),
        P(PAIR, None, None),
        P(PAIR, None),
        P(OCC, PAIR, None, None),
        P(OCC, PAIR, None),
        P(OCC, PAIR, None),
    )
    out_specs = (P(PAIR, None, None), P(PAIR, None, None))
    return jax.shard_map(local, mesh=grid, in_specs=in_specs, out_specs=out_specs, check_vma=False)
```

```python
import jax
import jax.numpy as jnp
from jax import lax
from jax.experimental import pallas as pl
from jax.experimental.pallas import tpu as pltpu
from jax.sharding import Mesh
from jax.sharding import PartitionSpec as P

F32, BF16 = jnp.float32, jnp.bfloat16
NZ, NY, NX, NC = 8, 4, 4, 2
OWNERS, PEERS = NZ * NY, NX * NC
N = 128
TILES = 4
DOMAIN = TILES * N
PAIRS = 8
ROWS = PAIRS * N
CHUNK = 512
EARLY = 48
LEAD = 3
AXES = ("z", "y", "x", "core")
PAIR, OCC = ("z", "y"), ("x", "core")


def split(x):
    high = x.astype(BF16)
    return high, (x - high.astype(F32)).astype(BF16)


def push(src, dst, send, recv, device):
    return pltpu.make_async_remote_copy(
        src_ref=src, dst_ref=dst, send_sem=send, recv_sem=recv,
        device_id=device, device_id_type=pl.DeviceIdType.MESH,
    )


class Place:
    def __init__(self):
        self.z, self.y = lax.axis_index("z"), lax.axis_index("y")
        self.x, self.core = lax.axis_index("x"), lax.axis_index("core")
        self.occ = self.x * NC + self.core
        self.me = self.z * NY + self.y

    def z_to(self, d):
        return {"z": lax.rem(self.z + d + NZ, NZ)}

    def y_to(self, d):
        return {"y": lax.rem(self.y + d + NY, NY)}

    def peer(self, j):
        other = lax.rem(self.occ + j + PEERS, PEERS)
        return other, {"x": other // NC, "core": lax.rem(other, NC)}

    def x_to(self, d):
        other = lax.rem(self.x + d + NX, NX)
        return other, {"x": other}

    def partner(self):
        return {"core": 1 - self.core}

    def sign(self, k):
        return 2 * lax.rem(k, 2) - 1

    def row(self, k):
        return lax.rem(self.z + self.sign(k) * ((k + 1) // 2) + NZ, NZ)

    def slot(self, k, dy):
        return self.row(k) * NY + lax.rem(self.y + dy + NY, NY)


class Gather:
    def __init__(self, at, buf, base, rows, zs, zr, ys, yr):
        self.at, self.buf, self.base, self.rows = at, buf, base, rows
        self.zs, self.zr, self.ys, self.yr = zs, zr, ys, yr

    def piece(self, slot, half):
        n = self.rows if half is None else self.rows // 2
        return self.buf.at[slot, pl.ds(self.base + (n if half == 1 else 0), n)]

    def copy(self, axis, slot, half, index, d):
        part = self.piece(slot, half)
        if axis == "z":
            return push(part, part, self.zs.at[index], self.zr.at[index], self.at.z_to(d))
        return push(part, part, self.ys.at[index], self.yr.at[index], self.at.y_to(d))

    def along_z(self, k, slot, tail):
        at, d = self.at, -self.at.sign(k)

        @pl.when(k < 7)
        def _():
            self.copy("z", slot, None, (k,) + tail, d).wait_recv()

        @pl.when(k < 5)
        def _():
            self.copy("z", slot, None, (k + 2,) + tail, d).start()

        @pl.when(k == 5)
        def _():
            self.copy("z", slot, 0, (7,) + tail, -1).start()

        @pl.when(k == 6)
        def _():
            self.copy("z", slot, 1, (8,) + tail, 1).start()

        @pl.when(k == 7)
        def _():
            self.copy("z", slot, 0, (7,) + tail, -1).wait_recv()
            self.copy("z", slot, 1, (8,) + tail, 1).wait_recv()

    def both_z(self, slot, tail):
        self.copy("z", slot, None, (1,) + tail, -1).start()
        self.copy("z", slot, None, (2,) + tail, 1).start()

    def sent_z(self, tail):
        for k in range(1, 7):
            self.copy("z", 0, None, (k,) + tail, 1).wait_send()
        self.copy("z", 0, 0, (7,) + tail, 1).wait_send()
        self.copy("z", 0, 1, (8,) + tail, 1).wait_send()


class ZFirst(Gather):
    def start(self):
        self.both_z(self.at.me, ())
        self.both_y(0)

    def both_y(self, k):
        slot = self.at.slot(k, 0)
        self.copy("y", slot, None, (k, 0), -1).start()
        self.copy("y", slot, None, (k, 1), 1).start()

    def take_z(self, k):
        self.along_z(k, self.at.slot(k, 0), ())
        self.both_y(k)

    def take_y(self, k):
        slot = self.at.slot(k, 1)
        self.copy("y", slot, None, (k, 0), -1).wait_recv()
        self.copy("y", slot, 0, (k, 2), -1).start()
        slot = self.at.slot(k, -1)
        self.copy("y", slot, None, (k, 1), 1).wait_recv()
        self.copy("y", slot, 1, (k, 3), 1).start()

    def last_y(self, k):
        slot = self.at.slot(k, 2)
        self.copy("y", slot, 0, (k, 2), -1).wait_recv()
        self.copy("y", slot, 1, (k, 3), 1).wait_recv()

    def sent(self):
        self.sent_z(())

        @pl.loop(0, NZ)
        def _(k):
            for index, half in enumerate((None, None, 0, 1)):
                self.copy("y", 0, half, (k, index), 1).wait_send()


class YFirst(Gather):
    def start(self):
        me = self.at.me
        self.copy("y", me, None, (0,), -1).start()
        self.copy("y", me, None, (1,), 1).start()
        self.both_z(me, (0,))

    def take_y(self):
        slot = self.at.slot(0, 1)
        self.copy("y", slot, None, (0,), -1).wait_recv()
        self.copy("y", slot, 0, (2,), -1).start()
        self.both_z(slot, (1,))
        slot = self.at.slot(0, -1)
        self.copy("y", slot, None, (1,), 1).wait_recv()
        self.copy("y", slot, 1, (3,), 1).start()
        self.both_z(slot, (2,))
        slot = self.at.slot(0, 2)
        self.copy("y", slot, 0, (2,), -1).wait_recv()
        self.copy("y", slot, 1, (3,), 1).wait_recv()
        self.both_z(slot, (3,))

    def take_z(self, k):
        for j, dy in enumerate((0, 1, -1, 2)):
            self.along_z(k, self.at.slot(k, dy), (j,))

    def sent(self):
        for index, half in enumerate((None, None, 0, 1)):
            self.copy("y", 0, half, (index,), 1).wait_send()
        for j in range(NY):
            self.sent_z((j,))


class Spread:
    def __init__(self, at, out, into, send, recv):
        self.at, self.out, self.into, self.send, self.recv = at, out, into, send, recv

    def copy(self, j):
        other, device = self.at.peer(j)
        return push(self.out(other), self.into.at[self.at.occ], self.send.at[j], self.recv.at[j], device)

    def start(self):
        for j in range(1, PEERS):
            self.copy(j).start()

    def arrived(self):
        for j in range(1, PEERS):
            self.copy(j).wait_recv()

    def sent(self):
        for j in range(1, PEERS):
            self.copy(j).wait_send()


class Sums:
    def __init__(self, at, total, near, far, send, recv):
        self.at, self.total, self.near, self.far, self.send, self.recv = at, total, near, far, send, recv

    def inside(self, j):
        other = self.at.x_to(j)[0]
        source = self.total.at[other, 1 - self.at.core]
        return push(source, self.near.at[other], self.send.at[j], self.recv.at[j], self.at.partner())

    def outside(self, j):
        other, device = self.at.x_to(j)
        source = self.total.at[other, self.at.core]
        index = NX + j
        return push(source, self.far.at[self.at.x], self.send.at[index], self.recv.at[index], device)

    def run(self):
        at, order = self.at, (2, 1, 3, 0)
        for j in order:
            self.inside(j).start()
        for j in order:
            other = at.x_to(j)[0]
            self.inside(j).wait_recv()
            self.total[other, at.core] += self.near[other]
            if j:
                self.outside(j).start()
        out = self.total[at.x, at.core]
        for j in (1, 3, 2):
            self.outside(j).wait_recv()
            out += self.far[at.x_to(-j)[0]]
        for j in order:
            self.inside(j).wait_send()
            if j:
                self.outside(j).wait_send()
        return out


class Shares:
    def __init__(self, at, buf, send, recv):
        self.at, self.buf, self.send, self.recv = at, buf, send, recv

    def outside(self, j):
        block = self.buf.at[self.at.x, self.at.core]
        return push(block, block, self.send.at[j], self.recv.at[j], self.at.x_to(j)[1])

    def inside(self, j):
        index = NX + j
        block = self.buf.at[self.at.x_to(-j)[0], self.at.core]
        return push(block, block, self.send.at[index], self.recv.at[index], self.at.partner())

    def start(self):
        for j in (2, 1, 3):
            self.outside(j).start()
        self.inside(0).start()

    def arrived(self):
        for j in (1, 3, 2):
            self.outside(j).wait_recv()
            self.inside(j).start()
        for j in range(NX):
            self.inside(j).wait_recv()

    def sent(self):
        for j in range(NX):
            self.inside(j).wait_send()
            if j:
                self.outside(j).wait_send()


def kernel(
    amp_hbm, exch_hbm, energy_ref, shift_ref, coef_ref, tiles_ref, pair_ref, weight_ref,
    final_ref, residual_ref,
    flipped, straight, coef_all, turned, amp_all, amp_next, high, low, high_t, low_t, up_all, down_all, total,
    near, near_next, far, far_next, current_all, residual_all, table_out, table_in, table,
    amp_own, exch_own,
    own_sem, c_zs, c_zr, c_ys, c_yr, t_zs, t_zr, t_ys, t_yr,
    n_zs, n_zr, n_ys, n_yr, m_zs, m_zr, m_ys, m_yr, peer_send, peer_recv,
):
    at = Place()
    fetch = [
        pltpu.make_async_copy(amp_hbm.at[at.occ], amp_own, own_sem.at[0]),
        pltpu.make_async_copy(exch_hbm.at[at.occ], exch_own, own_sem.at[1]),
    ]
    for copy in fetch:
        copy.start()

    barrier = pltpu.get_barrier_semaphore()
    for device in (at.z_to(-1), at.z_to(1), at.y_to(-1), at.y_to(1)):
        pl.semaphore_signal(barrier, inc=1, device_id=device, device_id_type=pl.DeviceIdType.MESH)
    for j in range(1, PEERS):
        pl.semaphore_signal(barrier, inc=1, device_id=at.peer(j)[1], device_id_type=pl.DeviceIdType.MESH)

    def ordered(p, t):
        tile = jnp.zeros((N, N), F32)
        for b in range(TILES):
            same = jnp.where(tiles_ref[p, b] == t, 1.0, 0.0)
            tile += coef_ref[p, b * N : (b + 1) * N, :].astype(F32) * same
        return tile.astype(BF16)

    for t in range(TILES):
        coef_all[at.me, t * N : (t + 1) * N, :] = ordered(at.occ, t)
    lane = lax.broadcasted_iota(jnp.int32, (PAIRS, N), 1) * PAIRS
    for place in range(PAIRS):
        piece = jnp.zeros((PAIRS, N), F32)
        for c in range(pair_ref.shape[1]):
            named = jnp.broadcast_to(pair_ref[:, c : c + 1], (PAIRS, N)) == lane + place
            piece += jnp.where(named, jnp.broadcast_to(weight_ref[:, c : c + 1], (PAIRS, N)), 0.0)
        table_out[place] = piece
    table_in[at.occ] = table_out[at.occ]
    for copy in fetch:
        copy.wait()
    amp_all[at.me] = amp_own[...]
    pl.semaphore_wait(barrier, 4 + PEERS - 1)

    coefs = ZFirst(at, coef_all, 0, DOMAIN, c_zs, c_zr, c_ys, c_yr)
    amps = YFirst(at, amp_all, 0, N, t_zs, t_zr, t_ys, t_yr)
    tables = Spread(at, lambda other: table_out.at[other], table_in, peer_send.at[0], peer_recv.at[0])
    coefs.start()
    amps.start()
    tables.start()

    @pl.loop(0, PAIRS)
    def _(p):
        for t in range(TILES):
            tile = ordered(p, t)
            straight[t * N : (t + 1) * N, pl.ds(pl.multiple_of(p * N, N), N)] = tile
            flipped[pl.ds(pl.multiple_of(p * N, N), N), t * N : (t + 1) * N] = tile.T

    for k in range(1, LEAD):
        coefs.take_z(k)
    amps.take_y()
    coefs.take_y(0)
    for k in range(1, LEAD):
        amps.take_z(k)
    tables.arrived()
    weights = table_in[0]
    for other in range(1, PEERS):
        weights += table_in[other]
    for owner in range(OWNERS):
        table[owner] = jnp.broadcast_to(weights[:, owner : owner + 1], (PAIRS, N))

    def overlaps(base):
        for pair in range(0, NY, 2):
            theirs = jnp.concatenate([coef_all[base + pair], coef_all[base + pair + 1]], axis=1)
            for first in range(0, ROWS, CHUNK):
                rows = slice(first, first + CHUNK)
                s = jnp.dot(flipped[rows, :], theirs, preferred_element_type=F32)
                up, down = split(s)
                for i in range(2):
                    high[base + pair + i, rows, :] = up[:, i * N : (i + 1) * N]
                    low[base + pair + i, rows, :] = down[:, i * N : (i + 1) * N]
        for y in range(NY):
            for t in range(TILES):
                part = slice(t * N, (t + 1) * N)
                turned[y * N : (y + 1) * N, part] = coef_all[base + y, part, :].T
        theirs = pl.ds(pl.multiple_of(base * N, NY * N), NY * N)
        for first in range(0, ROWS, 2 * N):
            cols = slice(first, first + 2 * N)
            s = jnp.dot(turned[...], straight[:, cols], preferred_element_type=F32)
            high_t[theirs, cols], low_t[theirs, cols] = split(s)

    def couple(base, amplitudes):
        for y in range(NY):
            slot = base + y
            both = jnp.concatenate(split(amplitudes[slot]), axis=1)
            both = jnp.concatenate([both, both], axis=0)
            for first in range(0, ROWS, CHUNK):
                rows = slice(first, first + CHUNK)
                s = jnp.concatenate([high[slot, rows, :], low[slot, rows, :]], axis=1)
                u = jnp.dot(s, both, preferred_element_type=F32)
                u = (u[:, :N] + u[:, N:]).reshape(CHUNK // N, N, N)
                u = u * table[slot, first // N : (first + CHUNK) // N, :][:, None, :]
                up, down = split(u.reshape(CHUNK, N))
                up_all[rows, y * N : (y + 1) * N] = up
                down_all[rows, y * N : (y + 1) * N] = down
        theirs = pl.ds(pl.multiple_of(base * N, NY * N), NY * N)

        for p in range(PAIRS):
            own = slice(p * N, (p + 1) * N)
            left = jnp.concatenate([up_all[own, :], down_all[own, :]], axis=0)
            right = jnp.concatenate([high_t[theirs, own], low_t[theirs, own]], axis=1)
            out = jnp.dot(left, right, preferred_element_type=F32)
            out = out[:N] + out[N:]
            total[p // NC, p % NC] += out[:, :N] + out[:, N:]

    def denominator(p):
        line = jnp.broadcast_to(energy_ref[pl.ds(p, 1), :], (N, N))
        return line.T + line + shift_ref[p]

    total[...] = jnp.zeros_like(total)

    @pl.loop(0, NZ)
    def _(k):
        @pl.when(k + 1 < NZ)
        def _():
            coefs.take_y(k + 1)

        @pl.when(k + LEAD < NZ)
        def _():
            coefs.take_z(k + LEAD)
            amps.take_z(k + LEAD)

        coefs.last_y(k)
        base = at.row(k) * NY
        overlaps(base)
        couple(base, amp_all)

    coupled = Sums(at, total, near, far, peer_send.at[1], peer_recv.at[1]).run()
    below = denominator(at.occ)
    current = amp_own[...]
    current = current - (exch_own[...] + below * current - coupled) / below
    amp_next[at.me] = current
    current_all[at.occ] = current
    total[...] = jnp.zeros_like(total)

    late = ZFirst(at, amp_next, EARLY, N - EARLY, m_zs, m_zr, m_ys, m_yr)
    early = YFirst(at, amp_next, 0, EARLY, n_zs, n_zr, n_ys, n_yr)
    currents = Spread(at, lambda other: current_all.at[at.occ], current_all, peer_send.at[2], peer_recv.at[2])
    late.start()
    early.start()
    currents.start()
    for k in range(1, LEAD):
        late.take_z(k)
    early.take_y()
    late.take_y(0)
    for k in range(1, LEAD):
        early.take_z(k)

    @pl.loop(0, NZ)
    def _(k):
        @pl.when(k + 1 < NZ)
        def _():
            late.take_y(k + 1)

        @pl.when(k + LEAD < NZ)
        def _():
            late.take_z(k + LEAD)
            early.take_z(k + LEAD)

        late.last_y(k)
        couple(at.row(k) * NY, amp_next)

    coupled = Sums(at, total, near_next, far_next, peer_send.at[3], peer_recv.at[3]).run()
    current = current_all[at.occ]
    residual_all[at.x, at.core] = exch_own[...] + below * current - coupled
    residuals = Shares(at, residual_all, peer_send.at[4], peer_recv.at[4])
    residuals.start()

    @pl.loop(0, PAIRS)
    def _(p):
        final_ref[p] = denominator(p)

    currents.arrived()
    residuals.arrived()

    @pl.loop(0, PAIRS)
    def _(p):
        residual = residual_all[p // NC, lax.rem(p, NC)]
        residual_ref[p] = residual
        final_ref[p] = current_all[p] - residual / final_ref[p]

    for copies in (coefs, amps, tables, late, early, currents, residuals):
        copies.sent()


def gather_sems():
    dma = pltpu.SemaphoreType.DMA
    z_first = [dma((9,)), dma((9,)), dma((NZ, 4)), dma((NZ, 4))]
    y_first = [dma((9, NY)), dma((9, NY)), dma((4,)), dma((4,))]
    return z_first + y_first + y_first + z_first


def local(
    amplitudes,
    exchange_ints,
    pno_energy,
    pair_shift,
    coefficients,
    domain_tiles,
    couple_owner,
    couple_index,
    couple_weight,
):
    coupled_pair = couple_owner[0, :, :, 0] * PAIRS + couple_index[0]
    vmem, smem, hbm = (
        pl.BlockSpec(memory_space=s) for s in (pltpu.VMEM, pltpu.SMEM, pltpu.HBM)
    )
    block = (N, N)
    out = jax.ShapeDtypeStruct((PAIRS, N, N), F32)
    return pl.pallas_call(
        kernel,
        out_shape=(out, out),
        in_specs=[hbm, hbm, vmem, smem, vmem, smem, vmem, vmem],
        out_specs=(vmem, vmem),
        scratch_shapes=[
            pltpu.VMEM((ROWS, DOMAIN), BF16),
            pltpu.VMEM((DOMAIN, ROWS), BF16),
            pltpu.VMEM((OWNERS, DOMAIN, N), BF16),
            pltpu.VMEM((NY * N, DOMAIN), BF16),
            pltpu.VMEM((OWNERS,) + block, F32),
            pltpu.VMEM((OWNERS,) + block, F32),
            pltpu.VMEM((OWNERS, ROWS, N), BF16),
            pltpu.VMEM((OWNERS, ROWS, N), BF16),
            pltpu.VMEM((OWNERS * N, ROWS), BF16),
            pltpu.VMEM((OWNERS * N, ROWS), BF16),
            pltpu.VMEM((ROWS, NY * N), BF16),
            pltpu.VMEM((ROWS, NY * N), BF16),
            pltpu.VMEM((NX, NC) + block, F32),
            pltpu.VMEM((NX,) + block, F32),
            pltpu.VMEM((NX,) + block, F32),
            pltpu.VMEM((NX,) + block, F32),
            pltpu.VMEM((NX,) + block, F32),
            pltpu.VMEM((PAIRS,) + block, F32),
            pltpu.VMEM((NX, NC) + block, F32),
            pltpu.VMEM((PEERS, PAIRS, N), F32),
            pltpu.VMEM((PEERS, PAIRS, N), F32),
            pltpu.VMEM((OWNERS, PAIRS, N), F32),
            pltpu.VMEM(block, F32),
            pltpu.VMEM(block, F32),
            pltpu.SemaphoreType.DMA((2,)),
            *gather_sems(),
            pltpu.SemaphoreType.DMA((5, PEERS)),
            pltpu.SemaphoreType.DMA((5, PEERS)),
        ],
        compiler_params=pltpu.CompilerParams(
            collective_id=0, has_side_effects=True, vmem_limit_bytes=52 << 20
        ),
    )(
        amplitudes, exchange_ints, pno_energy, pair_shift, coefficients, domain_tiles,
        coupled_pair, couple_weight[0],
    )


def solution(mesh):
    grid = Mesh(mesh.devices.reshape(NZ, NY, NX, NC), AXES)
    in_specs = (
        P(PAIR, None, None),
        P(PAIR, None, None),
        P(PAIR, None),
        P(PAIR),
        P(PAIR, None, None),
        P(PAIR, None),
        P(OCC, PAIR, None, None),
        P(OCC, PAIR, None),
        P(OCC, PAIR, None),
    )
    out_specs = (P(PAIR, None, None), P(PAIR, None, None))
    return jax.shard_map(local, mesh=grid, in_specs=in_specs, out_specs=out_specs, check_vma=False)
```

```python
import jax
import jax.numpy as jnp
from jax import lax
from jax.experimental import pallas as pl
from jax.experimental.pallas import tpu as pltpu
from jax.sharding import Mesh
from jax.sharding import PartitionSpec as P

F32, BF16 = jnp.float32, jnp.bfloat16
NZ, NY, NX, NC = 8, 4, 4, 2
OWNERS, PEERS = NZ * NY, NX * NC
N = 128
TILES = 4
DOMAIN = TILES * N
PAIRS = 8
ROWS = PAIRS * N
CHUNK = 512
EARLY = 48
AXES = ("z", "y", "x", "core")
PAIR, OCC = ("z", "y"), ("x", "core")


def split(x):
    high = x.astype(BF16)
    return high, (x - high.astype(F32)).astype(BF16)


def push(src, dst, send, recv, device):
    return pltpu.make_async_remote_copy(
        src_ref=src, dst_ref=dst, send_sem=send, recv_sem=recv,
        device_id=device, device_id_type=pl.DeviceIdType.MESH,
    )


class Place:
    def __init__(self):
        self.z, self.y = lax.axis_index("z"), lax.axis_index("y")
        self.x, self.core = lax.axis_index("x"), lax.axis_index("core")
        self.occ = self.x * NC + self.core
        self.me = self.z * NY + self.y

    def z_to(self, d):
        return {"z": lax.rem(self.z + d + NZ, NZ)}

    def y_to(self, d):
        return {"y": lax.rem(self.y + d + NY, NY)}

    def peer(self, j):
        other = lax.rem(self.occ + j + PEERS, PEERS)
        return other, {"x": other // NC, "core": lax.rem(other, NC)}

    def x_to(self, d):
        other = lax.rem(self.x + d + NX, NX)
        return other, {"x": other}

    def partner(self):
        return {"core": 1 - self.core}

    def sign(self, k):
        return 2 * lax.rem(k, 2) - 1

    def row(self, k):
        return lax.rem(self.z + self.sign(k) * ((k + 1) // 2) + NZ, NZ)

    def slot(self, k, dy):
        return self.row(k) * NY + lax.rem(self.y + dy + NY, NY)


class Gather:
    def __init__(self, at, buf, base, rows, zs, zr, ys, yr):
        self.at, self.buf, self.base, self.rows = at, buf, base, rows
        self.zs, self.zr, self.ys, self.yr = zs, zr, ys, yr

    def piece(self, slot, half):
        n = self.rows if half is None else self.rows // 2
        return self.buf.at[slot, pl.ds(self.base + (n if half == 1 else 0), n)]

    def copy(self, axis, slot, half, index, d):
        part = self.piece(slot, half)
        if axis == "z":
            return push(part, part, self.zs.at[index], self.zr.at[index], self.at.z_to(d))
        return push(part, part, self.ys.at[index], self.yr.at[index], self.at.y_to(d))

    def along_z(self, k, slot, tail):
        at, d = self.at, -self.at.sign(k)

        @pl.when(k < 7)
        def _():
            self.copy("z", slot, None, (k,) + tail, d).wait_recv()

        @pl.when(k < 5)
        def _():
            self.copy("z", slot, None, (k + 2,) + tail, d).start()

        @pl.when(k == 5)
        def _():
            self.copy("z", slot, 0, (7,) + tail, -1).start()

        @pl.when(k == 6)
        def _():
            self.copy("z", slot, 1, (8,) + tail, 1).start()

        @pl.when(k == 7)
        def _():
            self.copy("z", slot, 0, (7,) + tail, -1).wait_recv()
            self.copy("z", slot, 1, (8,) + tail, 1).wait_recv()

    def both_z(self, slot, tail):
        self.copy("z", slot, None, (1,) + tail, -1).start()
        self.copy("z", slot, None, (2,) + tail, 1).start()

    def sent_z(self, tail):
        for k in range(1, 7):
            self.copy("z", 0, None, (k,) + tail, 1).wait_send()
        self.copy("z", 0, 0, (7,) + tail, 1).wait_send()
        self.copy("z", 0, 1, (8,) + tail, 1).wait_send()


class ZFirst(Gather):
    def start(self):
        self.both_z(self.at.me, ())
        self.both_y(0)

    def both_y(self, k):
        slot = self.at.slot(k, 0)
        self.copy("y", slot, None, (k, 0), -1).start()
        self.copy("y", slot, None, (k, 1), 1).start()

    def take_z(self, k):
        self.along_z(k, self.at.slot(k, 0), ())
        self.both_y(k)

    def take_y(self, k):
        slot = self.at.slot(k, 1)
        self.copy("y", slot, None, (k, 0), -1).wait_recv()
        self.copy("y", slot, 0, (k, 2), -1).start()
        slot = self.at.slot(k, -1)
        self.copy("y", slot, None, (k, 1), 1).wait_recv()
        self.copy("y", slot, 1, (k, 3), 1).start()

    def last_y(self, k):
        slot = self.at.slot(k, 2)
        self.copy("y", slot, 0, (k, 2), -1).wait_recv()
        self.copy("y", slot, 1, (k, 3), 1).wait_recv()

    def sent(self):
        self.sent_z(())

        @pl.loop(0, NZ)
        def _(k):
            for index, half in enumerate((None, None, 0, 1)):
                self.copy("y", 0, half, (k, index), 1).wait_send()


class YFirst(Gather):
    def start(self):
        me = self.at.me
        self.copy("y", me, None, (0,), -1).start()
        self.copy("y", me, None, (1,), 1).start()
        self.both_z(me, (0,))

    def take_y(self):
        slot = self.at.slot(0, 1)
        self.copy("y", slot, None, (0,), -1).wait_recv()
        self.copy("y", slot, 0, (2,), -1).start()
        self.both_z(slot, (1,))
        slot = self.at.slot(0, -1)
        self.copy("y", slot, None, (1,), 1).wait_recv()
        self.copy("y", slot, 1, (3,), 1).start()
        self.both_z(slot, (2,))

    def last_y(self):
        slot = self.at.slot(0, 2)
        self.copy("y", slot, 0, (2,), -1).wait_recv()
        self.copy("y", slot, 1, (3,), 1).wait_recv()
        self.both_z(slot, (3,))

    def take_z(self, k, ways):
        for j in ways:
            self.along_z(k, self.at.slot(k, (0, 1, -1, 2)[j]), (j,))

    def sent(self):
        for index, half in enumerate((None, None, 0, 1)):
            self.copy("y", 0, half, (index,), 1).wait_send()
        for j in range(NY):
            self.sent_z((j,))


def each(hop, do):
    for k in (2 * hop - 1, 2 * hop):
        pl.when(k < NZ)(lambda k=k: do(k))


def levels(z_first, y_first, work):
    z_first.take_z(1)
    z_first.take_z(2)
    y_first.take_y()
    z_first.take_y(0)

    def level(t):
        each(t - 1, z_first.take_y)
        pl.when(t <= NZ // 2)(lambda: each(t, z_first.take_z))
        each(t - 1, lambda k: y_first.take_z(k, (0, 1, 2)))

    level(2)
    y_first.last_y()
    z_first.last_y(0)
    work(0)

    @pl.loop(3, NZ // 2 + 2)
    def _(t):
        level(t)
        each(t - 2, lambda k: y_first.take_z(k, (3,)))
        each(t - 2, z_first.last_y)

        @pl.loop(2 * t - 5, 2 * t - 3)
        def _(k):
            work(k)

    y_first.take_z(NZ - 1, (3,))
    z_first.last_y(NZ - 1)
    work(NZ - 1)


class Spread:
    def __init__(self, at, out, into, send, recv):
        self.at, self.out, self.into, self.send, self.recv = at, out, into, send, recv

    def copy(self, j):
        other, device = self.at.peer(j)
        return push(self.out(other), self.into.at[self.at.occ], self.send.at[j], self.recv.at[j], device)

    def start(self):
        for j in range(1, PEERS):
            self.copy(j).start()

    def arrived(self):
        for j in range(1, PEERS):
            self.copy(j).wait_recv()

    def sent(self):
        for j in range(1, PEERS):
            self.copy(j).wait_send()


class Sums:
    def __init__(self, at, total, near, far, send, recv):
        self.at, self.total, self.near, self.far, self.send, self.recv = at, total, near, far, send, recv

    def inside(self, j):
        other = self.at.x_to(j)[0]
        source = self.total.at[other, 1 - self.at.core]
        return push(source, self.near.at[other], self.send.at[j], self.recv.at[j], self.at.partner())

    def outside(self, j):
        other, device = self.at.x_to(j)
        source = self.total.at[other, self.at.core]
        index = NX + j
        return push(source, self.far.at[self.at.x], self.send.at[index], self.recv.at[index], device)

    def run(self):
        at, order = self.at, (2, 1, 3, 0)
        for j in order:
            self.inside(j).start()
        for j in order:
            other = at.x_to(j)[0]
            self.inside(j).wait_recv()
            self.total[other, at.core] += self.near[other]
            if j:
                self.outside(j).start()
        out = self.total[at.x, at.core]
        for j in (1, 3, 2):
            self.outside(j).wait_recv()
            out += self.far[at.x_to(-j)[0]]
        for j in order:
            self.inside(j).wait_send()
            if j:
                self.outside(j).wait_send()
        return out


class Shares:
    def __init__(self, at, buf, send, recv):
        self.at, self.buf, self.send, self.recv = at, buf, send, recv

    def outside(self, j):
        block = self.buf.at[self.at.x, self.at.core]
        return push(block, block, self.send.at[j], self.recv.at[j], self.at.x_to(j)[1])

    def inside(self, j):
        index = NX + j
        block = self.buf.at[self.at.x_to(-j)[0], self.at.core]
        return push(block, block, self.send.at[index], self.recv.at[index], self.at.partner())

    def start(self):
        for j in (2, 1, 3):
            self.outside(j).start()
        self.inside(0).start()

    def arrived(self):
        for j in (1, 3, 2):
            self.outside(j).wait_recv()
            self.inside(j).start()
        for j in range(NX):
            self.inside(j).wait_recv()

    def sent(self):
        for j in range(NX):
            self.inside(j).wait_send()
            if j:
                self.outside(j).wait_send()


def kernel(
    amp_hbm, exch_hbm, energy_ref, shift_ref, coef_ref, tiles_ref, pair_ref, weight_ref,
    final_ref, residual_ref,
    flipped, straight, coef_all, turned, amp_all, amp_next, high, low, high_t, low_t, up_all, down_all, total,
    near, near_next, far, far_next, current_all, residual_all, table_out, table_in, table,
    amp_own, exch_own,
    own_sem, c_zs, c_zr, c_ys, c_yr, t_zs, t_zr, t_ys, t_yr,
    n_zs, n_zr, n_ys, n_yr, m_zs, m_zr, m_ys, m_yr, peer_send, peer_recv,
):
    at = Place()
    fetch = [
        pltpu.make_async_copy(amp_hbm.at[at.occ], amp_own, own_sem.at[0]),
        pltpu.make_async_copy(exch_hbm.at[at.occ], exch_own, own_sem.at[1]),
    ]
    for copy in fetch:
        copy.start()

    barrier = pltpu.get_barrier_semaphore()
    for device in (at.z_to(-1), at.z_to(1), at.y_to(-1), at.y_to(1)):
        pl.semaphore_signal(barrier, inc=1, device_id=device, device_id_type=pl.DeviceIdType.MESH)
    for j in range(1, PEERS):
        pl.semaphore_signal(barrier, inc=1, device_id=at.peer(j)[1], device_id_type=pl.DeviceIdType.MESH)

    def ordered(p, t):
        tile = jnp.zeros((N, N), F32)
        for b in range(TILES):
            same = jnp.where(tiles_ref[p, b] == t, 1.0, 0.0)
            tile += coef_ref[p, b * N : (b + 1) * N, :].astype(F32) * same
        return tile.astype(BF16)

    for t in range(TILES):
        coef_all[at.me, t * N : (t + 1) * N, :] = ordered(at.occ, t)
    lane = lax.broadcasted_iota(jnp.int32, (PAIRS, N), 1) * PAIRS
    for place in range(PAIRS):
        piece = jnp.zeros((PAIRS, N), F32)
        for c in range(pair_ref.shape[1]):
            named = jnp.broadcast_to(pair_ref[:, c : c + 1], (PAIRS, N)) == lane + place
            piece += jnp.where(named, jnp.broadcast_to(weight_ref[:, c : c + 1], (PAIRS, N)), 0.0)
        table_out[place] = piece
    table_in[at.occ] = table_out[at.occ]
    for copy in fetch:
        copy.wait()
    amp_all[at.me] = amp_own[...]
    pl.semaphore_wait(barrier, 4 + PEERS - 1)

    coefs = ZFirst(at, coef_all, 0, DOMAIN, c_zs, c_zr, c_ys, c_yr)
    amps = YFirst(at, amp_all, 0, N, t_zs, t_zr, t_ys, t_yr)
    tables = Spread(at, lambda other: table_out.at[other], table_in, peer_send.at[0], peer_recv.at[0])
    coefs.start()
    amps.start()
    tables.start()

    @pl.loop(0, PAIRS)
    def _(p):
        for t in range(TILES):
            tile = ordered(p, t)
            straight[t * N : (t + 1) * N, pl.ds(pl.multiple_of(p * N, N), N)] = tile
            flipped[pl.ds(pl.multiple_of(p * N, N), N), t * N : (t + 1) * N] = tile.T

    tables.arrived()
    weights = table_in[0]
    for other in range(1, PEERS):
        weights += table_in[other]
    for owner in range(OWNERS):
        table[owner] = jnp.broadcast_to(weights[:, owner : owner + 1], (PAIRS, N))

    def overlaps(base):
        for pair in range(0, NY, 2):
            theirs = jnp.concatenate([coef_all[base + pair], coef_all[base + pair + 1]], axis=1)
            for first in range(0, ROWS, CHUNK):
                rows = slice(first, first + CHUNK)
                s = jnp.dot(flipped[rows, :], theirs, preferred_element_type=F32)
                up, down = split(s)
                for i in range(2):
                    high[base + pair + i, rows, :] = up[:, i * N : (i + 1) * N]
                    low[base + pair + i, rows, :] = down[:, i * N : (i + 1) * N]
        for y in range(NY):
            for t in range(TILES):
                part = slice(t * N, (t + 1) * N)
                turned[y * N : (y + 1) * N, part] = coef_all[base + y, part, :].T
        theirs = pl.ds(pl.multiple_of(base * N, NY * N), NY * N)
        for first in range(0, ROWS, 2 * N):
            cols = slice(first, first + 2 * N)
            s = jnp.dot(turned[...], straight[:, cols], preferred_element_type=F32)
            high_t[theirs, cols], low_t[theirs, cols] = split(s)

    def couple(base, amplitudes):
        for y in range(NY):
            slot = base + y
            both = jnp.concatenate(split(amplitudes[slot]), axis=1)
            both = jnp.concatenate([both, both], axis=0)
            for first in range(0, ROWS, CHUNK):
                rows = slice(first, first + CHUNK)
                s = jnp.concatenate([high[slot, rows, :], low[slot, rows, :]], axis=1)
                u = jnp.dot(s, both, preferred_element_type=F32)
                u = (u[:, :N] + u[:, N:]).reshape(CHUNK // N, N, N)
                u = u * table[slot, first // N : (first + CHUNK) // N, :][:, None, :]
                up, down = split(u.reshape(CHUNK, N))
                up_all[rows, y * N : (y + 1) * N] = up
                down_all[rows, y * N : (y + 1) * N] = down
        theirs = pl.ds(pl.multiple_of(base * N, NY * N), NY * N)

        for p in range(PAIRS):
            own = slice(p * N, (p + 1) * N)
            left = jnp.concatenate([up_all[own, :], down_all[own, :]], axis=0)
            right = jnp.concatenate([high_t[theirs, own], low_t[theirs, own]], axis=1)
            out = jnp.dot(left, right, preferred_element_type=F32)
            out = out[:N] + out[N:]
            total[p // NC, p % NC] += out[:, :N] + out[:, N:]

    def denominator(p):
        line = jnp.broadcast_to(energy_ref[pl.ds(p, 1), :], (N, N))
        return line.T + line + shift_ref[p]

    total[...] = jnp.zeros_like(total)

    def first(k):
        base = at.row(k) * NY
        overlaps(base)
        couple(base, amp_all)

    levels(coefs, amps, first)

    coupled = Sums(at, total, near, far, peer_send.at[1], peer_recv.at[1]).run()
    below = denominator(at.occ)
    current = amp_own[...]
    current = current - (exch_own[...] + below * current - coupled) / below
    amp_next[at.me] = current
    current_all[at.occ] = current
    total[...] = jnp.zeros_like(total)

    late = ZFirst(at, amp_next, EARLY, N - EARLY, m_zs, m_zr, m_ys, m_yr)
    early = YFirst(at, amp_next, 0, EARLY, n_zs, n_zr, n_ys, n_yr)
    currents = Spread(at, lambda other: current_all.at[at.occ], current_all, peer_send.at[2], peer_recv.at[2])
    late.start()
    early.start()
    currents.start()
    levels(late, early, lambda k: couple(at.row(k) * NY, amp_next))
    coupled = Sums(at, total, near_next, far_next, peer_send.at[3], peer_recv.at[3]).run()
    current = current_all[at.occ]
    residual_all[at.x, at.core] = exch_own[...] + below * current - coupled
    residuals = Shares(at, residual_all, peer_send.at[4], peer_recv.at[4])
    residuals.start()

    @pl.loop(0, PAIRS)
    def _(p):
        final_ref[p] = denominator(p)

    currents.arrived()
    residuals.arrived()

    @pl.loop(0, PAIRS)
    def _(p):
        residual = residual_all[p // NC, lax.rem(p, NC)]
        residual_ref[p] = residual
        final_ref[p] = current_all[p] - residual / final_ref[p]

    for copies in (coefs, amps, tables, late, early, currents, residuals):
        copies.sent()


def gather_sems():
    dma = pltpu.SemaphoreType.DMA
    z_first = [dma((9,)), dma((9,)), dma((NZ, 4)), dma((NZ, 4))]
    y_first = [dma((9, NY)), dma((9, NY)), dma((4,)), dma((4,))]
    return z_first + y_first + y_first + z_first


def local(
    amplitudes,
    exchange_ints,
    pno_energy,
    pair_shift,
    coefficients,
    domain_tiles,
    couple_owner,
    couple_index,
    couple_weight,
):
    coupled_pair = couple_owner[0, :, :, 0] * PAIRS + couple_index[0]
    vmem, smem, hbm = (
        pl.BlockSpec(memory_space=s) for s in (pltpu.VMEM, pltpu.SMEM, pltpu.HBM)
    )
    block = (N, N)
    out = jax.ShapeDtypeStruct((PAIRS, N, N), F32)
    return pl.pallas_call(
        kernel,
        out_shape=(out, out),
        in_specs=[hbm, hbm, vmem, smem, vmem, smem, vmem, vmem],
        out_specs=(vmem, vmem),
        scratch_shapes=[
            pltpu.VMEM((ROWS, DOMAIN), BF16),
            pltpu.VMEM((DOMAIN, ROWS), BF16),
            pltpu.VMEM((OWNERS, DOMAIN, N), BF16),
            pltpu.VMEM((NY * N, DOMAIN), BF16),
            pltpu.VMEM((OWNERS,) + block, F32),
            pltpu.VMEM((OWNERS,) + block, F32),
            pltpu.VMEM((OWNERS, ROWS, N), BF16),
            pltpu.VMEM((OWNERS, ROWS, N), BF16),
            pltpu.VMEM((OWNERS * N, ROWS), BF16),
            pltpu.VMEM((OWNERS * N, ROWS), BF16),
            pltpu.VMEM((ROWS, NY * N), BF16),
            pltpu.VMEM((ROWS, NY * N), BF16),
            pltpu.VMEM((NX, NC) + block, F32),
            pltpu.VMEM((NX,) + block, F32),
            pltpu.VMEM((NX,) + block, F32),
            pltpu.VMEM((NX,) + block, F32),
            pltpu.VMEM((NX,) + block, F32),
            pltpu.VMEM((PAIRS,) + block, F32),
            pltpu.VMEM((NX, NC) + block, F32),
            pltpu.VMEM((PEERS, PAIRS, N), F32),
            pltpu.VMEM((PEERS, PAIRS, N), F32),
            pltpu.VMEM((OWNERS, PAIRS, N), F32),
            pltpu.VMEM(block, F32),
            pltpu.VMEM(block, F32),
            pltpu.SemaphoreType.DMA((2,)),
            *gather_sems(),
            pltpu.SemaphoreType.DMA((5, PEERS)),
            pltpu.SemaphoreType.DMA((5, PEERS)),
        ],
        compiler_params=pltpu.CompilerParams(
            collective_id=0, has_side_effects=True, vmem_limit_bytes=52 << 20
        ),
    )(
        amplitudes, exchange_ints, pno_energy, pair_shift, coefficients, domain_tiles,
        coupled_pair, couple_weight[0],
    )


def solution(mesh):
    grid = Mesh(mesh.devices.reshape(NZ, NY, NX, NC), AXES)
    in_specs = (
        P(PAIR, None, None),
        P(PAIR, None, None),
        P(PAIR, None),
        P(PAIR),
        P(PAIR, None, None),
        P(PAIR, None),
        P(OCC, PAIR, None, None),
        P(OCC, PAIR, None),
        P(OCC, PAIR, None),
    )
    out_specs = (P(PAIR, None, None), P(PAIR, None, None))
    return jax.shard_map(local, mesh=grid, in_specs=in_specs, out_specs=out_specs, check_vma=False)
```

```python
import jax
import jax.numpy as jnp
from jax import lax
from jax.experimental import pallas as pl
from jax.experimental.pallas import tpu as pltpu
from jax.sharding import Mesh
from jax.sharding import PartitionSpec as P

F32, BF16 = jnp.float32, jnp.bfloat16
NZ, NY, NX, NC = 8, 4, 4, 2
OWNERS, PEERS = NZ * NY, NX * NC
N = 128
TILES = 4
DOMAIN = TILES * N
PAIRS = 8
ROWS = PAIRS * N
CHUNK = 512
EARLY = 48
AXES = ("z", "y", "x", "core")
PAIR, OCC = ("z", "y"), ("x", "core")


def split(x):
    high = x.astype(BF16)
    return high, (x - high.astype(F32)).astype(BF16)


def push(src, dst, send, recv, device):
    return pltpu.make_async_remote_copy(
        src_ref=src, dst_ref=dst, send_sem=send, recv_sem=recv,
        device_id=device, device_id_type=pl.DeviceIdType.MESH,
    )


class Place:
    def __init__(self):
        self.z, self.y = lax.axis_index("z"), lax.axis_index("y")
        self.x, self.core = lax.axis_index("x"), lax.axis_index("core")
        self.occ = self.x * NC + self.core
        self.me = self.z * NY + self.y

    def z_to(self, d):
        return {"z": lax.rem(self.z + d + NZ, NZ)}

    def y_to(self, d):
        return {"y": lax.rem(self.y + d + NY, NY)}

    def peer(self, j):
        other = lax.rem(self.occ + j + PEERS, PEERS)
        return other, {"x": other // NC, "core": lax.rem(other, NC)}

    def x_to(self, d):
        other = lax.rem(self.x + d + NX, NX)
        return other, {"x": other}

    def partner(self):
        return {"core": 1 - self.core}

    def sign(self, k):
        return 2 * lax.rem(k, 2) - 1

    def row(self, k):
        return lax.rem(self.z + self.sign(k) * ((k + 1) // 2) + NZ, NZ)

    def slot(self, k, dy):
        return self.row(k) * NY + lax.rem(self.y + dy + NY, NY)


class Gather:
    def __init__(self, at, buf, base, rows, zs, zr, ys, yr):
        self.at, self.buf, self.base, self.rows = at, buf, base, rows
        self.zs, self.zr, self.ys, self.yr = zs, zr, ys, yr

    def piece(self, slot, half):
        n = self.rows if half is None else self.rows // 2
        return self.buf.at[slot, pl.ds(self.base + (n if half == 1 else 0), n)]

    def copy(self, axis, slot, half, index, d):
        part = self.piece(slot, half)
        if axis == "z":
            return push(part, part, self.zs.at[index], self.zr.at[index], self.at.z_to(d))
        return push(part, part, self.ys.at[index], self.yr.at[index], self.at.y_to(d))

    def along_z(self, k, slot, tail):
        at, d = self.at, -self.at.sign(k)

        @pl.when(k < 7)
        def _():
            self.copy("z", slot, None, (k,) + tail, d).wait_recv()

        @pl.when(k < 5)
        def _():
            self.copy("z", slot, None, (k + 2,) + tail, d).start()

        @pl.when(k == 5)
        def _():
            self.copy("z", slot, 0, (7,) + tail, -1).start()

        @pl.when(k == 6)
        def _():
            self.copy("z", slot, 1, (8,) + tail, 1).start()

        @pl.when(k == 7)
        def _():
            self.copy("z", slot, 0, (7,) + tail, -1).wait_recv()
            self.copy("z", slot, 1, (8,) + tail, 1).wait_recv()

    def both_z(self, slot, tail):
        self.copy("z", slot, None, (1,) + tail, -1).start()
        self.copy("z", slot, None, (2,) + tail, 1).start()

    def sent_z(self, tail):
        for k in range(1, 7):
            self.copy("z", 0, None, (k,) + tail, 1).wait_send()
        self.copy("z", 0, 0, (7,) + tail, 1).wait_send()
        self.copy("z", 0, 1, (8,) + tail, 1).wait_send()


class ZFirst(Gather):
    def start(self):
        self.both_z(self.at.me, ())
        self.both_y(0)

    def both_y(self, k):
        slot = self.at.slot(k, 0)
        self.copy("y", slot, None, (k, 0), -1).start()
        self.copy("y", slot, None, (k, 1), 1).start()

    def take_z(self, k):
        self.along_z(k, self.at.slot(k, 0), ())
        self.both_y(k)

    def take_y(self, k):
        slot = self.at.slot(k, 1)
        self.copy("y", slot, None, (k, 0), -1).wait_recv()
        self.copy("y", slot, 0, (k, 2), -1).start()
        slot = self.at.slot(k, -1)
        self.copy("y", slot, None, (k, 1), 1).wait_recv()
        self.copy("y", slot, 1, (k, 3), 1).start()

    def last_y(self, k):
        slot = self.at.slot(k, 2)
        self.copy("y", slot, 0, (k, 2), -1).wait_recv()
        self.copy("y", slot, 1, (k, 3), 1).wait_recv()

    def sent(self):
        self.sent_z(())

        @pl.loop(0, NZ)
        def _(k):
            for index, half in enumerate((None, None, 0, 1)):
                self.copy("y", 0, half, (k, index), 1).wait_send()


class YFirst(Gather):
    def start(self):
        me = self.at.me
        self.copy("y", me, None, (0,), -1).start()
        self.copy("y", me, None, (1,), 1).start()
        self.both_z(me, (0,))

    def take_y(self):
        slot = self.at.slot(0, 1)
        self.copy("y", slot, None, (0,), -1).wait_recv()
        self.copy("y", slot, 0, (2,), -1).start()
        self.both_z(slot, (1,))
        slot = self.at.slot(0, -1)
        self.copy("y", slot, None, (1,), 1).wait_recv()
        self.copy("y", slot, 1, (3,), 1).start()
        self.both_z(slot, (2,))

    def last_y(self):
        slot = self.at.slot(0, 2)
        self.copy("y", slot, 0, (2,), -1).wait_recv()
        self.copy("y", slot, 1, (3,), 1).wait_recv()
        self.both_z(slot, (3,))

    def take_z(self, k, ways):
        for j in ways:
            self.along_z(k, self.at.slot(k, (0, 1, -1, 2)[j]), (j,))

    def sent(self):
        for index, half in enumerate((None, None, 0, 1)):
            self.copy("y", 0, half, (index,), 1).wait_send()
        for j in range(NY):
            self.sent_z((j,))


def each(hop, do):
    for k in (2 * hop - 1, 2 * hop):
        pl.when(k < NZ)(lambda k=k: do(k))


def levels(z_first, y_first, work):
    z_first.take_z(1)
    z_first.take_z(2)
    y_first.take_y()
    z_first.take_y(0)

    def level(t):
        pl.when(t <= NZ // 2)(lambda: each(t, z_first.take_z))
        each(t - 1, z_first.take_y)
        each(t - 1, lambda k: y_first.take_z(k, (0, 1, 2)))

    level(2)
    y_first.last_y()
    z_first.last_y(0)
    work(0)

    @pl.loop(3, NZ // 2 + 2)
    def _(t):
        each(t - 2, lambda k: y_first.take_z(k, (3,)))
        level(t)
        each(t - 2, z_first.last_y)

        @pl.loop(2 * t - 5, 2 * t - 3)
        def _(k):
            work(k)

    y_first.take_z(NZ - 1, (3,))
    z_first.last_y(NZ - 1)
    work(NZ - 1)


class Spread:
    def __init__(self, at, out, into, send, recv):
        self.at, self.out, self.into, self.send, self.recv = at, out, into, send, recv

    def copy(self, j):
        other, device = self.at.peer(j)
        return push(self.out(other), self.into.at[self.at.occ], self.send.at[j], self.recv.at[j], device)

    def start(self):
        for j in range(1, PEERS):
            self.copy(j).start()

    def arrived(self):
        for j in range(1, PEERS):
            self.copy(j).wait_recv()

    def sent(self):
        for j in range(1, PEERS):
            self.copy(j).wait_send()


class Sums:
    def __init__(self, at, total, near, far, send, recv):
        self.at, self.total, self.near, self.far, self.send, self.recv = at, total, near, far, send, recv

    def inside(self, j):
        other = self.at.x_to(j)[0]
        source = self.total.at[other, 1 - self.at.core]
        return push(source, self.near.at[other], self.send.at[j], self.recv.at[j], self.at.partner())

    def outside(self, j):
        other, device = self.at.x_to(j)
        source = self.total.at[other, self.at.core]
        index = NX + j
        return push(source, self.far.at[self.at.x], self.send.at[index], self.recv.at[index], device)

    def run(self):
        at, order = self.at, (2, 1, 3, 0)
        for j in order:
            self.inside(j).start()
        for j in order:
            other = at.x_to(j)[0]
            self.inside(j).wait_recv()
            self.total[other, at.core] += self.near[other]
            if j:
                self.outside(j).start()
        out = self.total[at.x, at.core]
        for j in (1, 3, 2):
            self.outside(j).wait_recv()
            out += self.far[at.x_to(-j)[0]]
        for j in order:
            self.inside(j).wait_send()
            if j:
                self.outside(j).wait_send()
        return out


class Shares:
    def __init__(self, at, buf, send, recv):
        self.at, self.buf, self.send, self.recv = at, buf, send, recv

    def outside(self, j):
        block = self.buf.at[self.at.x, self.at.core]
        return push(block, block, self.send.at[j], self.recv.at[j], self.at.x_to(j)[1])

    def inside(self, j):
        index = NX + j
        block = self.buf.at[self.at.x_to(-j)[0], self.at.core]
        return push(block, block, self.send.at[index], self.recv.at[index], self.at.partner())

    def start(self):
        for j in (2, 1, 3):
            self.outside(j).start()
        self.inside(0).start()

    def arrived(self):
        for j in (1, 3, 2):
            self.outside(j).wait_recv()
            self.inside(j).start()
        for j in range(NX):
            self.inside(j).wait_recv()

    def sent(self):
        for j in range(NX):
            self.inside(j).wait_send()
            if j:
                self.outside(j).wait_send()


def kernel(
    amp_hbm, exch_hbm, energy_ref, shift_ref, coef_ref, tiles_ref, pair_ref, weight_ref,
    final_ref, residual_ref,
    flipped, straight, coef_all, turned, amp_all, amp_next, high, low, high_t, low_t, up_all, down_all, total,
    near, near_next, far, far_next, current_all, residual_all, table_out, table_in, table,
    amp_own, exch_own,
    own_sem, c_zs, c_zr, c_ys, c_yr, t_zs, t_zr, t_ys, t_yr,
    n_zs, n_zr, n_ys, n_yr, m_zs, m_zr, m_ys, m_yr, peer_send, peer_recv,
):
    at = Place()
    fetch = [
        pltpu.make_async_copy(amp_hbm.at[at.occ], amp_own, own_sem.at[0]),
        pltpu.make_async_copy(exch_hbm.at[at.occ], exch_own, own_sem.at[1]),
    ]
    for copy in fetch:
        copy.start()

    barrier = pltpu.get_barrier_semaphore()
    for device in (at.z_to(-1), at.z_to(1), at.y_to(-1), at.y_to(1)):
        pl.semaphore_signal(barrier, inc=1, device_id=device, device_id_type=pl.DeviceIdType.MESH)
    for j in range(1, PEERS):
        pl.semaphore_signal(barrier, inc=1, device_id=at.peer(j)[1], device_id_type=pl.DeviceIdType.MESH)

    def ordered(p, t):
        tile = jnp.zeros((N, N), F32)
        for b in range(TILES):
            same = jnp.where(tiles_ref[p, b] == t, 1.0, 0.0)
            tile += coef_ref[p, b * N : (b + 1) * N, :].astype(F32) * same
        return tile.astype(BF16)

    for t in range(TILES):
        coef_all[at.me, t * N : (t + 1) * N, :] = ordered(at.occ, t)
    lane = lax.broadcasted_iota(jnp.int32, (PAIRS, N), 1) * PAIRS
    for place in range(PAIRS):
        piece = jnp.zeros((PAIRS, N), F32)
        for c in range(pair_ref.shape[1]):
            named = jnp.broadcast_to(pair_ref[:, c : c + 1], (PAIRS, N)) == lane + place
            piece += jnp.where(named, jnp.broadcast_to(weight_ref[:, c : c + 1], (PAIRS, N)), 0.0)
        table_out[place] = piece
    table_in[at.occ] = table_out[at.occ]
    for copy in fetch:
        copy.wait()
    amp_all[at.me] = amp_own[...]
    pl.semaphore_wait(barrier, 4 + PEERS - 1)

    coefs = ZFirst(at, coef_all, 0, DOMAIN, c_zs, c_zr, c_ys, c_yr)
    amps = YFirst(at, amp_all, 0, N, t_zs, t_zr, t_ys, t_yr)
    tables = Spread(at, lambda other: table_out.at[other], table_in, peer_send.at[0], peer_recv.at[0])
    coefs.start()
    amps.start()
    tables.start()

    @pl.loop(0, PAIRS)
    def _(p):
        for t in range(TILES):
            tile = ordered(p, t)
            straight[t * N : (t + 1) * N, pl.ds(pl.multiple_of(p * N, N), N)] = tile
            flipped[pl.ds(pl.multiple_of(p * N, N), N), t * N : (t + 1) * N] = tile.T

    tables.arrived()
    weights = table_in[0]
    for other in range(1, PEERS):
        weights += table_in[other]
    for owner in range(OWNERS):
        table[owner] = jnp.broadcast_to(weights[:, owner : owner + 1], (PAIRS, N))

    def overlaps(base):
        for pair in range(0, NY, 2):
            theirs = jnp.concatenate([coef_all[base + pair], coef_all[base + pair + 1]], axis=1)
            for first in range(0, ROWS, CHUNK):
                rows = slice(first, first + CHUNK)
                s = jnp.dot(flipped[rows, :], theirs, preferred_element_type=F32)
                up, down = split(s)
                for i in range(2):
                    high[base + pair + i, rows, :] = up[:, i * N : (i + 1) * N]
                    low[base + pair + i, rows, :] = down[:, i * N : (i + 1) * N]
        for y in range(NY):
            for t in range(TILES):
                part = slice(t * N, (t + 1) * N)
                turned[y * N : (y + 1) * N, part] = coef_all[base + y, part, :].T
        theirs = pl.ds(pl.multiple_of(base * N, NY * N), NY * N)
        for first in range(0, ROWS, 2 * N):
            cols = slice(first, first + 2 * N)
            s = jnp.dot(turned[...], straight[:, cols], preferred_element_type=F32)
            high_t[theirs, cols], low_t[theirs, cols] = split(s)

    def couple(base, amplitudes):
        for y in range(NY):
            slot = base + y
            both = jnp.concatenate(split(amplitudes[slot]), axis=1)
            both = jnp.concatenate([both, both], axis=0)
            for first in range(0, ROWS, CHUNK):
                rows = slice(first, first + CHUNK)
                s = jnp.concatenate([high[slot, rows, :], low[slot, rows, :]], axis=1)
                u = jnp.dot(s, both, preferred_element_type=F32)
                u = (u[:, :N] + u[:, N:]).reshape(CHUNK // N, N, N)
                u = u * table[slot, first // N : (first + CHUNK) // N, :][:, None, :]
                up, down = split(u.reshape(CHUNK, N))
                up_all[rows, y * N : (y + 1) * N] = up
                down_all[rows, y * N : (y + 1) * N] = down
        theirs = pl.ds(pl.multiple_of(base * N, NY * N), NY * N)

        for p in range(PAIRS):
            own = slice(p * N, (p + 1) * N)
            left = jnp.concatenate([up_all[own, :], down_all[own, :]], axis=0)
            right = jnp.concatenate([high_t[theirs, own], low_t[theirs, own]], axis=1)
            out = jnp.dot(left, right, preferred_element_type=F32)
            out = out[:N] + out[N:]
            total[p // NC, p % NC] += out[:, :N] + out[:, N:]

    def denominator(p):
        line = jnp.broadcast_to(energy_ref[pl.ds(p, 1), :], (N, N))
        return line.T + line + shift_ref[p]

    total[...] = jnp.zeros_like(total)

    def first(k):
        base = at.row(k) * NY
        overlaps(base)
        couple(base, amp_all)

    levels(coefs, amps, first)

    coupled = Sums(at, total, near, far, peer_send.at[1], peer_recv.at[1]).run()
    below = denominator(at.occ)
    current = amp_own[...]
    current = current - (exch_own[...] + below * current - coupled) / below
    amp_next[at.me] = current
    current_all[at.occ] = current
    total[...] = jnp.zeros_like(total)

    late = ZFirst(at, amp_next, EARLY, N - EARLY, m_zs, m_zr, m_ys, m_yr)
    early = YFirst(at, amp_next, 0, EARLY, n_zs, n_zr, n_ys, n_yr)
    currents = Spread(at, lambda other: current_all.at[at.occ], current_all, peer_send.at[2], peer_recv.at[2])
    late.start()
    early.start()
    currents.start()
    levels(late, early, lambda k: couple(at.row(k) * NY, amp_next))
    coupled = Sums(at, total, near_next, far_next, peer_send.at[3], peer_recv.at[3]).run()
    current = current_all[at.occ]
    residual_all[at.x, at.core] = exch_own[...] + below * current - coupled
    residuals = Shares(at, residual_all, peer_send.at[4], peer_recv.at[4])
    residuals.start()

    @pl.loop(0, PAIRS)
    def _(p):
        final_ref[p] = denominator(p)

    currents.arrived()
    residuals.arrived()

    @pl.loop(0, PAIRS)
    def _(p):
        residual = residual_all[p // NC, lax.rem(p, NC)]
        residual_ref[p] = residual
        final_ref[p] = current_all[p] - residual / final_ref[p]

    for copies in (coefs, amps, tables, late, early, currents, residuals):
        copies.sent()


def gather_sems():
    dma = pltpu.SemaphoreType.DMA
    z_first = [dma((9,)), dma((9,)), dma((NZ, 4)), dma((NZ, 4))]
    y_first = [dma((9, NY)), dma((9, NY)), dma((4,)), dma((4,))]
    return z_first + y_first + y_first + z_first


def local(
    amplitudes,
    exchange_ints,
    pno_energy,
    pair_shift,
    coefficients,
    domain_tiles,
    couple_owner,
    couple_index,
    couple_weight,
):
    coupled_pair = couple_owner[0, :, :, 0] * PAIRS + couple_index[0]
    vmem, smem, hbm = (
        pl.BlockSpec(memory_space=s) for s in (pltpu.VMEM, pltpu.SMEM, pltpu.HBM)
    )
    block = (N, N)
    out = jax.ShapeDtypeStruct((PAIRS, N, N), F32)
    return pl.pallas_call(
        kernel,
        out_shape=(out, out),
        in_specs=[hbm, hbm, vmem, smem, vmem, smem, vmem, vmem],
        out_specs=(vmem, vmem),
        scratch_shapes=[
            pltpu.VMEM((ROWS, DOMAIN), BF16),
            pltpu.VMEM((DOMAIN, ROWS), BF16),
            pltpu.VMEM((OWNERS, DOMAIN, N), BF16),
            pltpu.VMEM((NY * N, DOMAIN), BF16),
            pltpu.VMEM((OWNERS,) + block, F32),
            pltpu.VMEM((OWNERS,) + block, F32),
            pltpu.VMEM((OWNERS, ROWS, N), BF16),
            pltpu.VMEM((OWNERS, ROWS, N), BF16),
            pltpu.VMEM((OWNERS * N, ROWS), BF16),
            pltpu.VMEM((OWNERS * N, ROWS), BF16),
            pltpu.VMEM((ROWS, NY * N), BF16),
            pltpu.VMEM((ROWS, NY * N), BF16),
            pltpu.VMEM((NX, NC) + block, F32),
            pltpu.VMEM((NX,) + block, F32),
            pltpu.VMEM((NX,) + block, F32),
            pltpu.VMEM((NX,) + block, F32),
            pltpu.VMEM((NX,) + block, F32),
            pltpu.VMEM((PAIRS,) + block, F32),
            pltpu.VMEM((NX, NC) + block, F32),
            pltpu.VMEM((PEERS, PAIRS, N), F32),
            pltpu.VMEM((PEERS, PAIRS, N), F32),
            pltpu.VMEM((OWNERS, PAIRS, N), F32),
            pltpu.VMEM(block, F32),
            pltpu.VMEM(block, F32),
            pltpu.SemaphoreType.DMA((2,)),
            *gather_sems(),
            pltpu.SemaphoreType.DMA((5, PEERS)),
            pltpu.SemaphoreType.DMA((5, PEERS)),
        ],
        compiler_params=pltpu.CompilerParams(
            collective_id=0, has_side_effects=True, vmem_limit_bytes=52 << 20
        ),
    )(
        amplitudes, exchange_ints, pno_energy, pair_shift, coefficients, domain_tiles,
        coupled_pair, couple_weight[0],
    )


def solution(mesh):
    grid = Mesh(mesh.devices.reshape(NZ, NY, NX, NC), AXES)
    in_specs = (
        P(PAIR, None, None),
        P(PAIR, None, None),
        P(PAIR, None),
        P(PAIR),
        P(PAIR, None, None),
        P(PAIR, None),
        P(OCC, PAIR, None, None),
        P(OCC, PAIR, None),
        P(OCC, PAIR, None),
    )
    out_specs = (P(PAIR, None, None), P(PAIR, None, None))
    return jax.shard_map(local, mesh=grid, in_specs=in_specs, out_specs=out_specs, check_vma=False)
```

```python
import jax
import jax.numpy as jnp
from jax import lax
from jax.experimental import pallas as pl
from jax.experimental.pallas import tpu as pltpu
from jax.sharding import Mesh
from jax.sharding import PartitionSpec as P

F32, BF16 = jnp.float32, jnp.bfloat16
NZ, NY, NX, NC = 8, 4, 4, 2
OWNERS, PEERS = NZ * NY, NX * NC
N = 128
TILES = 4
DOMAIN = TILES * N
PAIRS = 8
ROWS = PAIRS * N
CHUNK = 512
EARLY = 48
AXES = ("z", "y", "x", "core")
PAIR, OCC = ("z", "y"), ("x", "core")


def split(x):
    high = x.astype(BF16)
    return high, (x - high.astype(F32)).astype(BF16)


def push(src, dst, send, recv, device):
    return pltpu.make_async_remote_copy(
        src_ref=src, dst_ref=dst, send_sem=send, recv_sem=recv,
        device_id=device, device_id_type=pl.DeviceIdType.MESH,
    )


class Place:
    def __init__(self):
        self.z, self.y = lax.axis_index("z"), lax.axis_index("y")
        self.x, self.core = lax.axis_index("x"), lax.axis_index("core")
        self.occ = self.x * NC + self.core
        self.me = self.z * NY + self.y

    def z_to(self, d):
        return {"z": lax.rem(self.z + d + NZ, NZ)}

    def y_to(self, d):
        return {"y": lax.rem(self.y + d + NY, NY)}

    def peer(self, j):
        other = lax.rem(self.occ + j + PEERS, PEERS)
        return other, {"x": other // NC, "core": lax.rem(other, NC)}

    def x_to(self, d):
        other = lax.rem(self.x + d + NX, NX)
        return other, {"x": other}

    def partner(self):
        return {"core": 1 - self.core}

    def sign(self, k):
        return 2 * lax.rem(k, 2) - 1

    def row(self, k):
        return lax.rem(self.z + self.sign(k) * ((k + 1) // 2) + NZ, NZ)

    def slot(self, k, dy):
        return self.row(k) * NY + lax.rem(self.y + dy + NY, NY)


class Gather:
    def __init__(self, at, buf, base, rows, zs, zr, ys, yr):
        self.at, self.buf, self.base, self.rows = at, buf, base, rows
        self.zs, self.zr, self.ys, self.yr = zs, zr, ys, yr

    def piece(self, slot, half):
        n = self.rows if half is None else self.rows // 2
        return self.buf.at[slot, pl.ds(self.base + (n if half == 1 else 0), n)]

    def copy(self, axis, slot, half, index, d):
        part = self.piece(slot, half)
        if axis == "z":
            return push(part, part, self.zs.at[index], self.zr.at[index], self.at.z_to(d))
        return push(part, part, self.ys.at[index], self.yr.at[index], self.at.y_to(d))

    def along_z(self, k, slot, tail):
        at, d = self.at, -self.at.sign(k)

        @pl.when(k < 7)
        def _():
            self.copy("z", slot, None, (k,) + tail, d).wait_recv()

        @pl.when(k < 5)
        def _():
            self.copy("z", slot, None, (k + 2,) + tail, d).start()

        @pl.when(k == 5)
        def _():
            self.copy("z", slot, 0, (7,) + tail, -1).start()

        @pl.when(k == 6)
        def _():
            self.copy("z", slot, 1, (8,) + tail, 1).start()

        @pl.when(k == 7)
        def _():
            self.copy("z", slot, 0, (7,) + tail, -1).wait_recv()
            self.copy("z", slot, 1, (8,) + tail, 1).wait_recv()

    def both_z(self, slot, tail):
        self.copy("z", slot, None, (1,) + tail, -1).start()
        self.copy("z", slot, None, (2,) + tail, 1).start()

    def sent_z(self, tail):
        for k in range(1, 7):
            self.copy("z", 0, None, (k,) + tail, 1).wait_send()
        self.copy("z", 0, 0, (7,) + tail, 1).wait_send()
        self.copy("z", 0, 1, (8,) + tail, 1).wait_send()


class ZFirst(Gather):
    def start(self):
        self.both_z(self.at.me, ())
        self.both_y(0)

    def both_y(self, k):
        slot = self.at.slot(k, 0)
        self.copy("y", slot, None, (k, 0), -1).start()
        self.copy("y", slot, None, (k, 1), 1).start()

    def take_z(self, k):
        self.along_z(k, self.at.slot(k, 0), ())
        self.both_y(k)

    def take_y(self, k):
        slot = self.at.slot(k, 1)
        self.copy("y", slot, None, (k, 0), -1).wait_recv()
        self.copy("y", slot, 0, (k, 2), -1).start()
        slot = self.at.slot(k, -1)
        self.copy("y", slot, None, (k, 1), 1).wait_recv()
        self.copy("y", slot, 1, (k, 3), 1).start()

    def last_y(self, k):
        slot = self.at.slot(k, 2)
        self.copy("y", slot, 0, (k, 2), -1).wait_recv()
        self.copy("y", slot, 1, (k, 3), 1).wait_recv()

    def sent(self):
        self.sent_z(())

        @pl.loop(0, NZ)
        def _(k):
            for index, half in enumerate((None, None, 0, 1)):
                self.copy("y", 0, half, (k, index), 1).wait_send()


class YFirst(Gather):
    def start(self):
        me = self.at.me
        self.copy("y", me, None, (0,), -1).start()
        self.copy("y", me, None, (1,), 1).start()
        self.both_z(me, (0,))

    def take_y(self):
        slot = self.at.slot(0, 1)
        self.copy("y", slot, None, (0,), -1).wait_recv()
        self.copy("y", slot, 0, (2,), -1).start()
        self.both_z(slot, (1,))
        slot = self.at.slot(0, -1)
        self.copy("y", slot, None, (1,), 1).wait_recv()
        self.copy("y", slot, 1, (3,), 1).start()
        self.both_z(slot, (2,))

    def last_y(self):
        slot = self.at.slot(0, 2)
        self.copy("y", slot, 0, (2,), -1).wait_recv()
        self.copy("y", slot, 1, (3,), 1).wait_recv()
        self.both_z(slot, (3,))

    def take_z(self, k, ways):
        for j in ways:
            self.along_z(k, self.at.slot(k, (0, 1, -1, 2)[j]), (j,))

    def sent(self):
        for index, half in enumerate((None, None, 0, 1)):
            self.copy("y", 0, half, (index,), 1).wait_send()
        for j in range(NY):
            self.sent_z((j,))


def each(hop, do):
    for k in (2 * hop - 1, 2 * hop):
        pl.when(k < NZ)(lambda k=k: do(k))


def levels(z_first, y_first, work):
    z_first.take_z(1)
    z_first.take_z(2)
    y_first.take_y()
    z_first.take_y(0)

    def level(t):
        pl.when(t <= NZ // 2)(lambda: each(t, z_first.take_z))
        each(t - 1, z_first.take_y)
        each(t - 1, lambda k: y_first.take_z(k, (0, 1, 2)))

    level(2)
    y_first.last_y()
    z_first.last_y(0)
    work(0)

    @pl.loop(3, NZ // 2 + 2)
    def _(t):
        each(t - 2, lambda k: y_first.take_z(k, (3,)))
        level(t)
        each(t - 2, z_first.last_y)

        @pl.loop(2 * t - 5, 2 * t - 3)
        def _(k):
            work(k)

    y_first.take_z(NZ - 1, (3,))
    z_first.last_y(NZ - 1)
    work(NZ - 1)


class Spread:
    def __init__(self, at, out, into, send, recv):
        self.at, self.out, self.into, self.send, self.recv = at, out, into, send, recv

    def copy(self, j):
        other, device = self.at.peer(j)
        return push(self.out(other), self.into.at[self.at.occ], self.send.at[j], self.recv.at[j], device)

    def start(self):
        for j in range(1, PEERS):
            self.copy(j).start()

    def arrived(self):
        for j in range(1, PEERS):
            self.copy(j).wait_recv()

    def sent(self):
        for j in range(1, PEERS):
            self.copy(j).wait_send()


class Sums:
    def __init__(self, at, total, near, far, send, recv):
        self.at, self.total, self.near, self.far, self.send, self.recv = at, total, near, far, send, recv

    def inside(self, j):
        other = self.at.x_to(j)[0]
        source = self.total.at[other, 1 - self.at.core]
        return push(source, self.near.at[other], self.send.at[j], self.recv.at[j], self.at.partner())

    def outside(self, j):
        other, device = self.at.x_to(j)
        source = self.total.at[other, self.at.core]
        index = NX + j
        return push(source, self.far.at[self.at.x], self.send.at[index], self.recv.at[index], device)

    def run(self):
        at, order = self.at, (2, 1, 3, 0)
        for j in order:
            self.inside(j).start()
        for j in order:
            other = at.x_to(j)[0]
            self.inside(j).wait_recv()
            self.total[other, at.core] += self.near[other]
            if j:
                self.outside(j).start()
        out = self.total[at.x, at.core]
        for j in (1, 3, 2):
            self.outside(j).wait_recv()
            out += self.far[at.x_to(-j)[0]]
        for j in order:
            self.inside(j).wait_send()
            if j:
                self.outside(j).wait_send()
        return out


class Shares:
    def __init__(self, at, buf, send, recv):
        self.at, self.buf, self.send, self.recv = at, buf, send, recv

    def outside(self, j):
        block = self.buf.at[self.at.x, self.at.core]
        return push(block, block, self.send.at[j], self.recv.at[j], self.at.x_to(j)[1])

    def inside(self, j):
        index = NX + j
        block = self.buf.at[self.at.x_to(-j)[0], self.at.core]
        return push(block, block, self.send.at[index], self.recv.at[index], self.at.partner())

    def start(self):
        for j in (2, 1, 3):
            self.outside(j).start()
        self.inside(0).start()

    def arrived(self):
        for j in (1, 3, 2):
            self.outside(j).wait_recv()
            self.inside(j).start()
        for j in range(NX):
            self.inside(j).wait_recv()

    def sent(self):
        for j in range(NX):
            self.inside(j).wait_send()
            if j:
                self.outside(j).wait_send()


def kernel(
    amp_hbm, exch_hbm, energy_ref, shift_ref, coef_ref, tiles_ref, pair_ref, weight_ref,
    final_ref, residual_ref,
    flipped, straight, coef_all, turned, amp_all, amp_next, high, low, high_t, low_t, up_all, down_all, total,
    near, near_next, far, far_next, current_all, residual_all, table_out, table_in, table,
    amp_own, exch_own,
    own_sem, c_zs, c_zr, c_ys, c_yr, t_zs, t_zr, t_ys, t_yr,
    n_zs, n_zr, n_ys, n_yr, m_zs, m_zr, m_ys, m_yr, peer_send, peer_recv,
):
    at = Place()
    fetch = [
        pltpu.make_async_copy(amp_hbm.at[at.occ], amp_own, own_sem.at[0]),
        pltpu.make_async_copy(exch_hbm.at[at.occ], exch_own, own_sem.at[1]),
    ]
    for copy in fetch:
        copy.start()

    barrier = pltpu.get_barrier_semaphore()
    for device in (at.z_to(-1), at.z_to(1), at.y_to(-1), at.y_to(1)):
        pl.semaphore_signal(barrier, inc=1, device_id=device, device_id_type=pl.DeviceIdType.MESH)
    for j in range(1, PEERS):
        pl.semaphore_signal(barrier, inc=1, device_id=at.peer(j)[1], device_id_type=pl.DeviceIdType.MESH)

    def ordered(p, t):
        tile = jnp.zeros((N, N), F32)
        for b in range(TILES):
            same = jnp.where(tiles_ref[p, b] == t, 1.0, 0.0)
            tile += coef_ref[p, b * N : (b + 1) * N, :].astype(F32) * same
        return tile.astype(BF16)

    for t in range(TILES):
        coef_all[at.me, t * N : (t + 1) * N, :] = ordered(at.occ, t)
    coefs = ZFirst(at, coef_all, 0, DOMAIN, c_zs, c_zr, c_ys, c_yr)
    amps = YFirst(at, amp_all, 0, N, t_zs, t_zr, t_ys, t_yr)
    tables = Spread(at, lambda other: table_out.at[other], table_in, peer_send.at[0], peer_recv.at[0])
    for copy in fetch:
        copy.wait()
    amp_all[at.me] = amp_own[...]
    pl.semaphore_wait(barrier, 4 + PEERS - 1)
    coefs.start()
    amps.start()

    lane = lax.broadcasted_iota(jnp.int32, (PAIRS, N), 1) * PAIRS
    for place in range(PAIRS):
        piece = jnp.zeros((PAIRS, N), F32)
        for c in range(pair_ref.shape[1]):
            named = jnp.broadcast_to(pair_ref[:, c : c + 1], (PAIRS, N)) == lane + place
            piece += jnp.where(named, jnp.broadcast_to(weight_ref[:, c : c + 1], (PAIRS, N)), 0.0)
        table_out[place] = piece
    table_in[at.occ] = table_out[at.occ]
    tables.start()

    @pl.loop(0, PAIRS)
    def _(p):
        for t in range(TILES):
            tile = ordered(p, t)
            straight[t * N : (t + 1) * N, pl.ds(pl.multiple_of(p * N, N), N)] = tile
            flipped[pl.ds(pl.multiple_of(p * N, N), N), t * N : (t + 1) * N] = tile.T

    tables.arrived()
    weights = table_in[0]
    for other in range(1, PEERS):
        weights += table_in[other]
    for owner in range(OWNERS):
        table[owner] = jnp.broadcast_to(weights[:, owner : owner + 1], (PAIRS, N))

    def overlaps(base):
        for pair in range(0, NY, 2):
            theirs = jnp.concatenate([coef_all[base + pair], coef_all[base + pair + 1]], axis=1)
            for first in range(0, ROWS, CHUNK):
                rows = slice(first, first + CHUNK)
                s = jnp.dot(flipped[rows, :], theirs, preferred_element_type=F32)
                up, down = split(s)
                for i in range(2):
                    high[base + pair + i, rows, :] = up[:, i * N : (i + 1) * N]
                    low[base + pair + i, rows, :] = down[:, i * N : (i + 1) * N]
        for y in range(NY):
            for t in range(TILES):
                part = slice(t * N, (t + 1) * N)
                turned[y * N : (y + 1) * N, part] = coef_all[base + y, part, :].T
        theirs = pl.ds(pl.multiple_of(base * N, NY * N), NY * N)
        for first in range(0, ROWS, 2 * N):
            cols = slice(first, first + 2 * N)
            s = jnp.dot(turned[...], straight[:, cols], preferred_element_type=F32)
            high_t[theirs, cols], low_t[theirs, cols] = split(s)

    def couple(base, amplitudes):
        for y in range(NY):
            slot = base + y
            both = jnp.concatenate(split(amplitudes[slot]), axis=1)
            both = jnp.concatenate([both, both], axis=0)
            for first in range(0, ROWS, CHUNK):
                rows = slice(first, first + CHUNK)
                s = jnp.concatenate([high[slot, rows, :], low[slot, rows, :]], axis=1)
                u = jnp.dot(s, both, preferred_element_type=F32)
                u = (u[:, :N] + u[:, N:]).reshape(CHUNK // N, N, N)
                u = u * table[slot, first // N : (first + CHUNK) // N, :][:, None, :]
                up, down = split(u.reshape(CHUNK, N))
                up_all[rows, y * N : (y + 1) * N] = up
                down_all[rows, y * N : (y + 1) * N] = down
        theirs = pl.ds(pl.multiple_of(base * N, NY * N), NY * N)

        for p in range(PAIRS):
            own = slice(p * N, (p + 1) * N)
            left = jnp.concatenate([up_all[own, :], down_all[own, :]], axis=0)
            right = jnp.concatenate([high_t[theirs, own], low_t[theirs, own]], axis=1)
            out = jnp.dot(left, right, preferred_element_type=F32)
            out = out[:N] + out[N:]
            total[p // NC, p % NC] += out[:, :N] + out[:, N:]

    def denominator(p):
        line = jnp.broadcast_to(energy_ref[pl.ds(p, 1), :], (N, N))
        return line.T + line + shift_ref[p]

    total[...] = jnp.zeros_like(total)

    def first(k):
        base = at.row(k) * NY
        overlaps(base)
        couple(base, amp_all)

    levels(coefs, amps, first)

    coupled = Sums(at, total, near, far, peer_send.at[1], peer_recv.at[1]).run()
    below = denominator(at.occ)
    current = amp_own[...]
    current = current - (exch_own[...] + below * current - coupled) / below
    amp_next[at.me] = current
    current_all[at.occ] = current
    total[...] = jnp.zeros_like(total)

    late = ZFirst(at, amp_next, EARLY, N - EARLY, m_zs, m_zr, m_ys, m_yr)
    early = YFirst(at, amp_next, 0, EARLY, n_zs, n_zr, n_ys, n_yr)
    currents = Spread(at, lambda other: current_all.at[at.occ], current_all, peer_send.at[2], peer_recv.at[2])
    late.start()
    early.start()
    currents.start()
    levels(late, early, lambda k: couple(at.row(k) * NY, amp_next))
    coupled = Sums(at, total, near_next, far_next, peer_send.at[3], peer_recv.at[3]).run()
    current = current_all[at.occ]
    residual_all[at.x, at.core] = exch_own[...] + below * current - coupled
    residuals = Shares(at, residual_all, peer_send.at[4], peer_recv.at[4])
    residuals.start()

    @pl.loop(0, PAIRS)
    def _(p):
        final_ref[p] = denominator(p)

    currents.arrived()
    residuals.arrived()

    @pl.loop(0, PAIRS)
    def _(p):
        residual = residual_all[p // NC, lax.rem(p, NC)]
        residual_ref[p] = residual
        final_ref[p] = current_all[p] - residual / final_ref[p]

    for copies in (coefs, amps, tables, late, early, currents, residuals):
        copies.sent()


def gather_sems():
    dma = pltpu.SemaphoreType.DMA
    z_first = [dma((9,)), dma((9,)), dma((NZ, 4)), dma((NZ, 4))]
    y_first = [dma((9, NY)), dma((9, NY)), dma((4,)), dma((4,))]
    return z_first + y_first + y_first + z_first


def local(
    amplitudes,
    exchange_ints,
    pno_energy,
    pair_shift,
    coefficients,
    domain_tiles,
    couple_owner,
    couple_index,
    couple_weight,
):
    coupled_pair = couple_owner[0, :, :, 0] * PAIRS + couple_index[0]
    vmem, smem, hbm = (
        pl.BlockSpec(memory_space=s) for s in (pltpu.VMEM, pltpu.SMEM, pltpu.HBM)
    )
    block = (N, N)
    out = jax.ShapeDtypeStruct((PAIRS, N, N), F32)
    return pl.pallas_call(
        kernel,
        out_shape=(out, out),
        in_specs=[hbm, hbm, vmem, smem, vmem, smem, vmem, vmem],
        out_specs=(vmem, vmem),
        scratch_shapes=[
            pltpu.VMEM((ROWS, DOMAIN), BF16),
            pltpu.VMEM((DOMAIN, ROWS), BF16),
            pltpu.VMEM((OWNERS, DOMAIN, N), BF16),
            pltpu.VMEM((NY * N, DOMAIN), BF16),
            pltpu.VMEM((OWNERS,) + block, F32),
            pltpu.VMEM((OWNERS,) + block, F32),
            pltpu.VMEM((OWNERS, ROWS, N), BF16),
            pltpu.VMEM((OWNERS, ROWS, N), BF16),
            pltpu.VMEM((OWNERS * N, ROWS), BF16),
            pltpu.VMEM((OWNERS * N, ROWS), BF16),
            pltpu.VMEM((ROWS, NY * N), BF16),
            pltpu.VMEM((ROWS, NY * N), BF16),
            pltpu.VMEM((NX, NC) + block, F32),
            pltpu.VMEM((NX,) + block, F32),
            pltpu.VMEM((NX,) + block, F32),
            pltpu.VMEM((NX,) + block, F32),
            pltpu.VMEM((NX,) + block, F32),
            pltpu.VMEM((PAIRS,) + block, F32),
            pltpu.VMEM((NX, NC) + block, F32),
            pltpu.VMEM((PEERS, PAIRS, N), F32),
            pltpu.VMEM((PEERS, PAIRS, N), F32),
            pltpu.VMEM((OWNERS, PAIRS, N), F32),
            pltpu.VMEM(block, F32),
            pltpu.VMEM(block, F32),
            pltpu.SemaphoreType.DMA((2,)),
            *gather_sems(),
            pltpu.SemaphoreType.DMA((5, PEERS)),
            pltpu.SemaphoreType.DMA((5, PEERS)),
        ],
        compiler_params=pltpu.CompilerParams(
            collective_id=0, has_side_effects=True, vmem_limit_bytes=52 << 20
        ),
    )(
        amplitudes, exchange_ints, pno_energy, pair_shift, coefficients, domain_tiles,
        coupled_pair, couple_weight[0],
    )


def solution(mesh):
    grid = Mesh(mesh.devices.reshape(NZ, NY, NX, NC), AXES)
    in_specs = (
        P(PAIR, None, None),
        P(PAIR, None, None),
        P(PAIR, None),
        P(PAIR),
        P(PAIR, None, None),
        P(PAIR, None),
        P(OCC, PAIR, None, None),
        P(OCC, PAIR, None),
        P(OCC, PAIR, None),
    )
    out_specs = (P(PAIR, None, None), P(PAIR, None, None))
    return jax.shard_map(local, mesh=grid, in_specs=in_specs, out_specs=out_specs, check_vma=False)
```

```python
import jax
import jax.numpy as jnp
from jax import lax
from jax.experimental import pallas as pl
from jax.experimental.pallas import tpu as pltpu
from jax.sharding import Mesh
from jax.sharding import PartitionSpec as P

F32, BF16 = jnp.float32, jnp.bfloat16
NZ, NY, NX, NC = 8, 4, 4, 2
OWNERS, PEERS = NZ * NY, NX * NC
N = 128
TILES = 4
DOMAIN = TILES * N
PAIRS = 8
ROWS = PAIRS * N
CHUNK = 512
EARLY = 48
AXES = ("z", "y", "x", "core")
PAIR, OCC = ("z", "y"), ("x", "core")


def split(x):
    high = x.astype(BF16)
    return high, (x - high.astype(F32)).astype(BF16)


def push(src, dst, send, recv, device):
    return pltpu.make_async_remote_copy(
        src_ref=src, dst_ref=dst, send_sem=send, recv_sem=recv,
        device_id=device, device_id_type=pl.DeviceIdType.MESH,
    )


class Place:
    def __init__(self):
        self.z, self.y = lax.axis_index("z"), lax.axis_index("y")
        self.x, self.core = lax.axis_index("x"), lax.axis_index("core")
        self.occ = self.x * NC + self.core
        self.me = self.z * NY + self.y

    def z_to(self, d):
        return {"z": lax.rem(self.z + d + NZ, NZ)}

    def y_to(self, d):
        return {"y": lax.rem(self.y + d + NY, NY)}

    def peer(self, j):
        other = lax.rem(self.occ + j + PEERS, PEERS)
        return other, {"x": other // NC, "core": lax.rem(other, NC)}

    def x_to(self, d):
        other = lax.rem(self.x + d + NX, NX)
        return other, {"x": other}

    def partner(self):
        return {"core": 1 - self.core}

    def sign(self, k):
        return 2 * lax.rem(k, 2) - 1

    def row(self, k):
        return lax.rem(self.z + self.sign(k) * ((k + 1) // 2) + NZ, NZ)

    def slot(self, k, dy):
        return self.row(k) * NY + lax.rem(self.y + dy + NY, NY)


class Gather:
    def __init__(self, at, buf, base, rows, zs, zr, ys, yr):
        self.at, self.buf, self.base, self.rows = at, buf, base, rows
        self.zs, self.zr, self.ys, self.yr = zs, zr, ys, yr

    def piece(self, slot, half):
        n = self.rows if half is None else self.rows // 2
        return self.buf.at[slot, pl.ds(self.base + (n if half == 1 else 0), n)]

    def copy(self, axis, slot, half, index, d):
        part = self.piece(slot, half)
        if axis == "z":
            return push(part, part, self.zs.at[index], self.zr.at[index], self.at.z_to(d))
        return push(part, part, self.ys.at[index], self.yr.at[index], self.at.y_to(d))

    def along_z(self, k, slot, tail):
        at, d = self.at, -self.at.sign(k)

        @pl.when(k < 7)
        def _():
            self.copy("z", slot, None, (k,) + tail, d).wait_recv()

        @pl.when(k < 5)
        def _():
            self.copy("z", slot, None, (k + 2,) + tail, d).start()

        @pl.when(k == 5)
        def _():
            self.copy("z", slot, 0, (7,) + tail, -1).start()

        @pl.when(k == 6)
        def _():
            self.copy("z", slot, 1, (8,) + tail, 1).start()

        @pl.when(k == 7)
        def _():
            self.copy("z", slot, 0, (7,) + tail, -1).wait_recv()
            self.copy("z", slot, 1, (8,) + tail, 1).wait_recv()

    def both_z(self, slot, tail):
        self.copy("z", slot, None, (1,) + tail, -1).start()
        self.copy("z", slot, None, (2,) + tail, 1).start()

    def sent_z(self, tail):
        for k in range(1, 7):
            self.copy("z", 0, None, (k,) + tail, 1).wait_send()
        self.copy("z", 0, 0, (7,) + tail, 1).wait_send()
        self.copy("z", 0, 1, (8,) + tail, 1).wait_send()


class ZFirst(Gather):
    def start(self):
        self.both_z(self.at.me, ())
        self.both_y(0)

    def both_y(self, k):
        slot = self.at.slot(k, 0)
        self.copy("y", slot, None, (k, 0), -1).start()
        self.copy("y", slot, None, (k, 1), 1).start()

    def take_z(self, k):
        self.along_z(k, self.at.slot(k, 0), ())
        self.both_y(k)

    def take_y(self, k):
        slot = self.at.slot(k, 1)
        self.copy("y", slot, None, (k, 0), -1).wait_recv()
        self.copy("y", slot, 0, (k, 2), -1).start()
        slot = self.at.slot(k, -1)
        self.copy("y", slot, None, (k, 1), 1).wait_recv()
        self.copy("y", slot, 1, (k, 3), 1).start()

    def last_y(self, k):
        slot = self.at.slot(k, 2)
        self.copy("y", slot, 0, (k, 2), -1).wait_recv()
        self.copy("y", slot, 1, (k, 3), 1).wait_recv()

    def sent(self):
        self.sent_z(())

        @pl.loop(0, NZ)
        def _(k):
            for index, half in enumerate((None, None, 0, 1)):
                self.copy("y", 0, half, (k, index), 1).wait_send()


class YFirst(Gather):
    def start(self):
        me = self.at.me
        self.copy("y", me, None, (0,), -1).start()
        self.copy("y", me, None, (1,), 1).start()
        self.both_z(me, (0,))

    def take_y(self):
        slot = self.at.slot(0, 1)
        self.copy("y", slot, None, (0,), -1).wait_recv()
        self.copy("y", slot, 0, (2,), -1).start()
        self.both_z(slot, (1,))
        slot = self.at.slot(0, -1)
        self.copy("y", slot, None, (1,), 1).wait_recv()
        self.copy("y", slot, 1, (3,), 1).start()
        self.both_z(slot, (2,))

    def last_y(self):
        slot = self.at.slot(0, 2)
        self.copy("y", slot, 0, (2,), -1).wait_recv()
        self.copy("y", slot, 1, (3,), 1).wait_recv()
        self.both_z(slot, (3,))

    def take_z(self, k, ways):
        for j in ways:
            self.along_z(k, self.at.slot(k, (0, 1, -1, 2)[j]), (j,))

    def sent(self):
        for index, half in enumerate((None, None, 0, 1)):
            self.copy("y", 0, half, (index,), 1).wait_send()
        for j in range(NY):
            self.sent_z((j,))


def each(hop, do):
    for k in (2 * hop - 1, 2 * hop):
        pl.when(k < NZ)(lambda k=k: do(k))


def levels(z_first, y_first, work):
    z_first.take_z(1)
    z_first.take_z(2)
    y_first.take_y()
    z_first.take_y(0)

    def level(t):
        pl.when(t <= NZ // 2)(lambda: each(t, z_first.take_z))
        each(t - 1, z_first.take_y)
        each(t - 1, lambda k: y_first.take_z(k, (0, 1, 2)))

    level(2)
    y_first.last_y()
    z_first.last_y(0)
    work(0)

    @pl.loop(3, NZ // 2 + 2)
    def _(t):
        each(t - 2, lambda k: y_first.take_z(k, (3,)))
        level(t)
        each(t - 2, z_first.last_y)

        @pl.loop(2 * t - 5, 2 * t - 3)
        def _(k):
            work(k)

    y_first.take_z(NZ - 1, (3,))
    z_first.last_y(NZ - 1)
    work(NZ - 1)


class Spread:
    def __init__(self, at, out, into, send, recv):
        self.at, self.out, self.into, self.send, self.recv = at, out, into, send, recv

    def copy(self, j):
        other, device = self.at.peer(j)
        return push(self.out(other), self.into.at[self.at.occ], self.send.at[j], self.recv.at[j], device)

    def start(self):
        for j in range(1, PEERS):
            self.copy(j).start()

    def arrived(self):
        for j in range(1, PEERS):
            self.copy(j).wait_recv()

    def sent(self):
        for j in range(1, PEERS):
            self.copy(j).wait_send()


class Sums:
    def __init__(self, at, total, near, far, send, recv):
        self.at, self.total, self.near, self.far, self.send, self.recv = at, total, near, far, send, recv

    def inside(self, j):
        other = self.at.x_to(j)[0]
        source = self.total.at[other, 1 - self.at.core]
        return push(source, self.near.at[other], self.send.at[j], self.recv.at[j], self.at.partner())

    def outside(self, j):
        other, device = self.at.x_to(j)
        source = self.total.at[other, self.at.core]
        index = NX + j
        return push(source, self.far.at[self.at.x], self.send.at[index], self.recv.at[index], device)

    def run(self):
        at, order = self.at, (2, 1, 3, 0)
        for j in order:
            self.inside(j).start()
        for j in order:
            other = at.x_to(j)[0]
            self.inside(j).wait_recv()
            self.total[other, at.core] += self.near[other]
            if j:
                self.outside(j).start()
        out = self.total[at.x, at.core]
        for j in (1, 3, 2):
            self.outside(j).wait_recv()
            out += self.far[at.x_to(-j)[0]]
        for j in order:
            self.inside(j).wait_send()
            if j:
                self.outside(j).wait_send()
        return out


class Shares:
    def __init__(self, at, buf, send, recv):
        self.at, self.buf, self.send, self.recv = at, buf, send, recv

    def outside(self, j):
        block = self.buf.at[self.at.x, self.at.core]
        return push(block, block, self.send.at[j], self.recv.at[j], self.at.x_to(j)[1])

    def inside(self, j):
        index = NX + j
        block = self.buf.at[self.at.x_to(-j)[0], self.at.core]
        return push(block, block, self.send.at[index], self.recv.at[index], self.at.partner())

    def start(self):
        for j in (2, 1, 3):
            self.outside(j).start()
        self.inside(0).start()

    def arrived(self):
        for j in (1, 3, 2):
            self.outside(j).wait_recv()
            self.inside(j).start()
        for j in range(NX):
            self.inside(j).wait_recv()

    def sent(self):
        for j in range(NX):
            self.inside(j).wait_send()
            if j:
                self.outside(j).wait_send()


def kernel(
    amp_hbm, exch_hbm, energy_ref, shift_ref, coef_ref, tiles_ref, pair_ref, weight_ref,
    current_ref, coupled_ref,
    flipped, straight, coef_all, turned, amp_all, amp_next, high, low, high_t, low_t, up_all, down_all, total,
    near, near_next, far, far_next, current_all, coupled_all, table_out, table_in, table,
    amp_own, exch_own,
    own_sem, c_zs, c_zr, c_ys, c_yr, t_zs, t_zr, t_ys, t_yr,
    n_zs, n_zr, n_ys, n_yr, m_zs, m_zr, m_ys, m_yr, peer_send, peer_recv,
):
    at = Place()
    fetch = [
        pltpu.make_async_copy(amp_hbm.at[at.occ], amp_own, own_sem.at[0]),
        pltpu.make_async_copy(exch_hbm.at[at.occ], exch_own, own_sem.at[1]),
    ]
    for copy in fetch:
        copy.start()

    barrier = pltpu.get_barrier_semaphore()
    for device in (at.z_to(-1), at.z_to(1), at.y_to(-1), at.y_to(1)):
        pl.semaphore_signal(barrier, inc=1, device_id=device, device_id_type=pl.DeviceIdType.MESH)
    for j in range(1, PEERS):
        pl.semaphore_signal(barrier, inc=1, device_id=at.peer(j)[1], device_id_type=pl.DeviceIdType.MESH)

    def ordered(p, t):
        tile = jnp.zeros((N, N), F32)
        for b in range(TILES):
            same = jnp.where(tiles_ref[p, b] == t, 1.0, 0.0)
            tile += coef_ref[p, b * N : (b + 1) * N, :].astype(F32) * same
        return tile.astype(BF16)

    for t in range(TILES):
        coef_all[at.me, t * N : (t + 1) * N, :] = ordered(at.occ, t)
    lane = lax.broadcasted_iota(jnp.int32, (PAIRS, N), 1) * PAIRS
    for place in range(PAIRS):
        piece = jnp.zeros((PAIRS, N), F32)
        for c in range(pair_ref.shape[1]):
            named = jnp.broadcast_to(pair_ref[:, c : c + 1], (PAIRS, N)) == lane + place
            piece += jnp.where(named, jnp.broadcast_to(weight_ref[:, c : c + 1], (PAIRS, N)), 0.0)
        table_out[place] = piece
    table_in[at.occ] = table_out[at.occ]
    for copy in fetch:
        copy.wait()
    amp_all[at.me] = amp_own[...]
    pl.semaphore_wait(barrier, 4 + PEERS - 1)

    coefs = ZFirst(at, coef_all, 0, DOMAIN, c_zs, c_zr, c_ys, c_yr)
    amps = YFirst(at, amp_all, 0, N, t_zs, t_zr, t_ys, t_yr)
    tables = Spread(at, lambda other: table_out.at[other], table_in, peer_send.at[0], peer_recv.at[0])
    coefs.start()
    amps.start()
    tables.start()

    @pl.loop(0, PAIRS)
    def _(p):
        for t in range(TILES):
            tile = ordered(p, t)
            straight[t * N : (t + 1) * N, pl.ds(pl.multiple_of(p * N, N), N)] = tile
            flipped[pl.ds(pl.multiple_of(p * N, N), N), t * N : (t + 1) * N] = tile.T

    tables.arrived()
    weights = table_in[0]
    for other in range(1, PEERS):
        weights += table_in[other]
    for owner in range(OWNERS):
        table[owner] = jnp.broadcast_to(weights[:, owner : owner + 1], (PAIRS, N))

    def overlaps(base):
        for pair in range(0, NY, 2):
            theirs = jnp.concatenate([coef_all[base + pair], coef_all[base + pair + 1]], axis=1)
            for first in range(0, ROWS, CHUNK):
                rows = slice(first, first + CHUNK)
                s = jnp.dot(flipped[rows, :], theirs, preferred_element_type=F32)
                up, down = split(s)
                for i in range(2):
                    high[base + pair + i, rows, :] = up[:, i * N : (i + 1) * N]
                    low[base + pair + i, rows, :] = down[:, i * N : (i + 1) * N]
        for y in range(NY):
            for t in range(TILES):
                part = slice(t * N, (t + 1) * N)
                turned[y * N : (y + 1) * N, part] = coef_all[base + y, part, :].T
        theirs = pl.ds(pl.multiple_of(base * N, NY * N), NY * N)
        for first in range(0, ROWS, 2 * N):
            cols = slice(first, first + 2 * N)
            s = jnp.dot(turned[...], straight[:, cols], preferred_element_type=F32)
            high_t[theirs, cols], low_t[theirs, cols] = split(s)

    def couple(base, amplitudes):
        for y in range(NY):
            slot = base + y
            both = jnp.concatenate(split(amplitudes[slot]), axis=1)
            both = jnp.concatenate([both, both], axis=0)
            for first in range(0, ROWS, CHUNK):
                rows = slice(first, first + CHUNK)
                s = jnp.concatenate([high[slot, rows, :], low[slot, rows, :]], axis=1)
                u = jnp.dot(s, both, preferred_element_type=F32)
                u = (u[:, :N] + u[:, N:]).reshape(CHUNK // N, N, N)
                u = u * table[slot, first // N : (first + CHUNK) // N, :][:, None, :]
                up, down = split(u.reshape(CHUNK, N))
                up_all[rows, y * N : (y + 1) * N] = up
                down_all[rows, y * N : (y + 1) * N] = down
        theirs = pl.ds(pl.multiple_of(base * N, NY * N), NY * N)

        for p in range(PAIRS):
            own = slice(p * N, (p + 1) * N)
            left = jnp.concatenate([up_all[own, :], down_all[own, :]], axis=0)
            right = jnp.concatenate([high_t[theirs, own], low_t[theirs, own]], axis=1)
            out = jnp.dot(left, right, preferred_element_type=F32)
            out = out[:N] + out[N:]
            total[p // NC, p % NC] += out[:, :N] + out[:, N:]

    def denominator(p):
        line = jnp.broadcast_to(energy_ref[pl.ds(p, 1), :], (N, N))
        return line.T + line + shift_ref[p]

    total[...] = jnp.zeros_like(total)

    def first(k):
        base = at.row(k) * NY
        overlaps(base)
        couple(base, amp_all)

    levels(coefs, amps, first)

    coupled = Sums(at, total, near, far, peer_send.at[1], peer_recv.at[1]).run()
    below = denominator(at.occ)
    current = amp_own[...]
    current = current - (exch_own[...] + below * current - coupled) / below
    amp_next[at.me] = current
    current_all[at.occ] = current
    total[...] = jnp.zeros_like(total)

    late = ZFirst(at, amp_next, EARLY, N - EARLY, m_zs, m_zr, m_ys, m_yr)
    early = YFirst(at, amp_next, 0, EARLY, n_zs, n_zr, n_ys, n_yr)
    currents = Spread(at, lambda other: current_all.at[at.occ], current_all, peer_send.at[2], peer_recv.at[2])
    late.start()
    early.start()
    currents.start()
    levels(late, early, lambda k: couple(at.row(k) * NY, amp_next))
    coupled = Sums(at, total, near_next, far_next, peer_send.at[3], peer_recv.at[3]).run()
    coupled_all[at.x, at.core] = coupled
    sums = Shares(at, coupled_all, peer_send.at[4], peer_recv.at[4])
    sums.start()
    currents.arrived()
    current_ref[...] = current_all[...]
    sums.arrived()
    for x in range(NX):
        for core in range(NC):
            coupled_ref[x * NC + core] = coupled_all[x, core]

    for copies in (coefs, amps, tables, late, early, currents, sums):
        copies.sent()


def gather_sems():
    dma = pltpu.SemaphoreType.DMA
    z_first = [dma((9,)), dma((9,)), dma((NZ, 4)), dma((NZ, 4))]
    y_first = [dma((9, NY)), dma((9, NY)), dma((4,)), dma((4,))]
    return z_first + y_first + y_first + z_first


def local(
    amplitudes,
    exchange_ints,
    pno_energy,
    pair_shift,
    coefficients,
    domain_tiles,
    couple_owner,
    couple_index,
    couple_weight,
):
    coupled_pair = couple_owner[0, :, :, 0] * PAIRS + couple_index[0]
    vmem, smem, hbm = (
        pl.BlockSpec(memory_space=s) for s in (pltpu.VMEM, pltpu.SMEM, pltpu.HBM)
    )
    block = (N, N)
    out = jax.ShapeDtypeStruct((PAIRS, N, N), F32)
    current, coupled = pl.pallas_call(
        kernel,
        out_shape=(out, out),
        in_specs=[hbm, hbm, vmem, smem, vmem, smem, vmem, vmem],
        out_specs=(vmem, vmem),
        scratch_shapes=[
            pltpu.VMEM((ROWS, DOMAIN), BF16),
            pltpu.VMEM((DOMAIN, ROWS), BF16),
            pltpu.VMEM((OWNERS, DOMAIN, N), BF16),
            pltpu.VMEM((NY * N, DOMAIN), BF16),
            pltpu.VMEM((OWNERS,) + block, F32),
            pltpu.VMEM((OWNERS,) + block, F32),
            pltpu.VMEM((OWNERS, ROWS, N), BF16),
            pltpu.VMEM((OWNERS, ROWS, N), BF16),
            pltpu.VMEM((OWNERS * N, ROWS), BF16),
            pltpu.VMEM((OWNERS * N, ROWS), BF16),
            pltpu.VMEM((ROWS, NY * N), BF16),
            pltpu.VMEM((ROWS, NY * N), BF16),
            pltpu.VMEM((NX, NC) + block, F32),
            pltpu.VMEM((NX,) + block, F32),
            pltpu.VMEM((NX,) + block, F32),
            pltpu.VMEM((NX,) + block, F32),
            pltpu.VMEM((NX,) + block, F32),
            pltpu.VMEM((PAIRS,) + block, F32),
            pltpu.VMEM((NX, NC) + block, F32),
            pltpu.VMEM((PEERS, PAIRS, N), F32),
            pltpu.VMEM((PEERS, PAIRS, N), F32),
            pltpu.VMEM((OWNERS, PAIRS, N), F32),
            pltpu.VMEM(block, F32),
            pltpu.VMEM(block, F32),
            pltpu.SemaphoreType.DMA((2,)),
            *gather_sems(),
            pltpu.SemaphoreType.DMA((5, PEERS)),
            pltpu.SemaphoreType.DMA((5, PEERS)),
        ],
        compiler_params=pltpu.CompilerParams(
            collective_id=0, has_side_effects=True, vmem_limit_bytes=52 << 20
        ),
    )(
        amplitudes, exchange_ints, pno_energy, pair_shift, coefficients, domain_tiles,
        coupled_pair, couple_weight[0],
    )
    denominator = pno_energy[:, :, None] + pno_energy[:, None, :] + pair_shift[:, None, None]
    residual = exchange_ints + denominator * current - coupled
    return current - residual / denominator, residual


def solution(mesh):
    grid = Mesh(mesh.devices.reshape(NZ, NY, NX, NC), AXES)
    in_specs = (
        P(PAIR, None, None),
        P(PAIR, None, None),
        P(PAIR, None),
        P(PAIR),
        P(PAIR, None, None),
        P(PAIR, None),
        P(OCC, PAIR, None, None),
        P(OCC, PAIR, None),
        P(OCC, PAIR, None),
    )
    out_specs = (P(PAIR, None, None), P(PAIR, None, None))
    return jax.shard_map(local, mesh=grid, in_specs=in_specs, out_specs=out_specs, check_vma=False)
```
